32 devices in a mesh: dp: 8 (over z, x), section: 4 (over y, core).
Axes of the slice: x: 2, y: 2, z: 4, core: 2. Of those that a mesh axis runs over, the one named last changes fastest.
Arguments:
- pieces: bfloat16 [2048, 7, 512], P(('dp', 'section')), may hold values from -6 to 6
- counts: int32 [2048], P(('dp', 'section')), may hold values from 1 to 7
- groups: int32 [2048], P(('dp', 'section')), may hold values from 0 to 7
- group_table: bfloat16 [8, 512], replicated, may hold values from -3 to 3
- attn_gain: bfloat16 [2, 512], replicated, may hold values from 0.5 to 1.5
- attn_qkv: bfloat16 [2, 512, 1536], replicated, may hold values from -0.25 to 0.25
- attn_out: bfloat16 [2, 512, 512], replicated, may hold values from -0.5 to 0.5
- attn_bias: bfloat16 [2, 512], replicated, may hold values from -2 to 2
- ffn_gain: bfloat16 [2, 512], replicated, may hold values from 0.5 to 1.5
- ffn_up: bfloat16 [2, 512, 2048], replicated, may hold values from -0.25 to 0.25
- ffn_up_bias: bfloat16 [2, 2048], replicated, may hold values from -3 to 3
- ffn_down: bfloat16 [2, 2048, 512], replicated, may hold values from -0.125 to 0.125
- ffn_down_bias: bfloat16 [2, 512], replicated, may hold values from -2 to 2
- final_gain: bfloat16 [512], replicated, may hold values from 0.5 to 1.5
- pool_weight: bfloat16 [512, 2048], replicated, may hold values from -0.25 to 0.25
- pool_bias: bfloat16 [2048], replicated, may hold values from -3 to 3
- emb_cotangent: bfloat16 [2048, 2048], P(('dp', 'section')), may hold values from -6 to 6
Outputs:
- embeddings: bfloat16 [2048, 2048], P(('dp', 'section'))
- input_grad: bfloat16 [2048, 7, 512], P(('dp', 'section'))
- table_grad: float32 [8, 512], P(None, 'dp')
- attn_gain_grad: float32 [2, 512], P(None, 'dp')
- attn_qkv_grad: float32 [2, 512, 1536], P(None, 'dp')
- attn_out_grad: float32 [2, 512, 512], P(None, 'dp')
- attn_bias_grad: float32 [2, 512], P(None, 'dp')
- ffn_gain_grad: float32 [2, 512], P(None, 'dp')
- ffn_up_grad: float32 [2, 512, 2048], P(None, 'dp')
- ffn_up_bias_grad: float32 [2, 2048], P(None, 'dp')
- ffn_down_grad: float32 [2, 2048, 512], P(None, 'dp')
- ffn_down_bias_grad: float32 [2, 512], P(None, 'dp')
- final_gain_grad: float32 [512], P('dp')
- pool_weight_grad: float32 [512, 2048], P('dp')
- pool_bias_grad: float32 [2048], P('dp')
The draws below stay inside these ranges and needn't reach their ends.
All inputs are finite; a program needn't handle non-finite values.
Results may differ from the reference program's by a relative error of at most 0.015.
Values may be sent and summed in bfloat16 or wider, within the bound.
A program may use at most 192 MiB of HBM per device.

```python
import jax
import jax.numpy as jnp
from jax import lax

D = 512
HEADS = 8
FF = 2048
PROJ = 2048
PIECES = 7
GROUPS = 8
LAYERS = 2
ENTRIES = 2048
N_DP = 8


def with_ends(array, stream_key, least, largest):
    dims = array.shape
    place = [jax.random.randint(jax.random.fold_in(stream_key, axis), (), 0, dims[axis]) for axis in range(len(dims))]
    array = array.at[tuple(place)].set(least)
    longest = dims.index(max(dims))
    place[longest] = (place[longest] + 1) % dims[longest]
    return array.at[tuple(place)].set(largest)


def raised(values, own_key, source, target, shards_of, factor):
    owner, partner = [(jnp.arange(values.shape[dim]) // (values.shape[dim] // shards_of)).reshape([-1 if axis == dim else 1 for axis in range(values.ndim)]) for dim in (source, target)]
    chosen = jax.random.permutation(own_key, shards_of)[partner]
    strong = (owner == chosen) | (owner == (partner + shards_of // 2) % shards_of)
    return jnp.where(strong, factor * values, values)


def block_levels(rng, shape, cuts, smallest, high):
    level, own = 1.0, jax.random.fold_in(rng, 6)
    for axis_at, blocks in cuts:
        draws = jnp.exp(jax.random.uniform(jax.random.fold_in(own, axis_at), (blocks,), jnp.float32, smallest / len(cuts), high / len(cuts)))
        level = level * jnp.repeat(draws, shape[axis_at] // blocks).reshape([-1 if axis == axis_at else 1 for axis in range(len(shape))])
    return level


def scatter_about(key, extent, deviation, most, cuts=(), kind=jnp.bfloat16):
    level = block_levels(key, extent, cuts, -0.22, 0.18) if cuts else 1.0
    values = jax.random.normal(key, extent, jnp.float32) * deviation * level
    return jnp.minimum(jnp.maximum(values, -most), most).astype(kind)


def heavy_noise(stream_key, dims, deviation, reach, split, heavy, dtype=jnp.bfloat16):
    values = deviation * jax.random.normal(stream_key, dims, jnp.float32)
    if split:
        values = values * block_levels(stream_key, dims, split, -0.22, 0.18)
    return jnp.clip(raised(values, jax.random.fold_in(stream_key, 3), *heavy), -reach, reach).astype(dtype)


def setup_inputs(seed: int = 0) -> dict:
    keys = jax.random.split(jax.random.key(seed), 18)
    return {
        "pieces": scatter_about(keys[0], (ENTRIES, PIECES, D), 1.0, 6.0, ((0, 32),)),
        "counts": with_ends(jax.random.randint(keys[1], (ENTRIES,), 1, PIECES + 1), jax.random.fold_in(keys[1], 1), 1, PIECES).astype(jnp.int32),
        "groups": with_ends(jax.random.randint(keys[2], (ENTRIES,), 0, GROUPS), jax.random.fold_in(keys[2], 1), 0, GROUPS - 1).astype(jnp.int32),
        "group_table": scatter_about(keys[3], (GROUPS, D), 0.5, 3.0),
        "attn_gain": jnp.clip(1.0 + 0.1 * jax.random.normal(keys[4], (LAYERS, D), jnp.float32), 0.5, 1.5).astype(jnp.bfloat16),
        "attn_qkv": scatter_about(keys[5], (LAYERS, D, 3 * D), D ** -0.5, 0.25),
        "attn_out": scatter_about(keys[6], (LAYERS, D, D), (D // 4) ** -0.5, 0.5),
        "attn_bias": scatter_about(keys[7], (LAYERS, D), 0.3, 2.0),
        "ffn_gain": jnp.clip(1.0 + 0.1 * jax.random.normal(keys[8], (LAYERS, D), jnp.float32), 0.5, 1.5).astype(jnp.bfloat16),
        "ffn_up": scatter_about(keys[9], (LAYERS, D, FF), D ** -0.5, 0.25),
        "ffn_up_bias": scatter_about(keys[10], (LAYERS, FF), 0.5, 3.0),
        "ffn_down": scatter_about(keys[11], (LAYERS, FF, D), FF ** -0.5, 0.125),
        "ffn_down_bias": scatter_about(keys[12], (LAYERS, D), 0.3, 2.0),
        "final_gain": jnp.clip(1.0 + 0.1 * jax.random.normal(keys[13], (D,), jnp.float32), 0.5, 1.5).astype(jnp.bfloat16),
        "pool_weight": scatter_about(keys[14], (D, PROJ), D ** -0.5, 0.25),
        "pool_bias": scatter_about(keys[15], (PROJ,), 0.5, 3.0),
        "emb_cotangent": heavy_noise(keys[16], (ENTRIES, PROJ), 1.0, 6.0, ((0, 32),), (0, 1, 32, 2.75)),
    }


@jax.custom_vjp
def low(v):
    return lax.optimization_barrier(v.astype(jnp.bfloat16)).astype(jnp.float32)

@jax.custom_vjp
def low_back(v):
    return v

def low_keep(v):
    return (low(v), None)

def low_pass(kept, grad):
    return (grad,)

def back_keep(v):
    return (v, None)

def back_low(kept, grad):
    return (low(grad),)
low.defvjp(low_keep, low_pass)
low_back.defvjp(back_keep, back_low)
EPS = 1e-05
MASKED = -1e+30
HIGH = lax.Precision.HIGHEST

def layer_norm(values, norm_gain):
    centre = values - lax.optimization_barrier(jnp.mean(values, axis=-1, keepdims=True))
    spread = lax.optimization_barrier(jnp.mean(centre * centre, axis=-1, keepdims=True))
    return centre * lax.rsqrt(spread + EPS) * norm_gain

def matmul_high(left_side, right_side):
    return jnp.dot(left_side, right_side, precision=HIGH, preferred_element_type=jnp.float32)

def pool_mean(hidden, live_mask, norm_gain):
    entries, pieces = live_mask.shape
    normed = layer_norm(hidden, norm_gain).reshape(entries, pieces, -1)
    return lax.optimization_barrier(jnp.sum(normed * live_mask[:, :, None], axis=1)) / lax.optimization_barrier(jnp.sum(live_mask, axis=1, keepdims=True))

def attention_half(hidden, live_mask, norm_gain, w_qkv, w_out, b_out):
    entries, pieces = live_mask.shape
    head_size = D // HEADS
    normed = low(layer_norm(hidden, norm_gain))
    projected = low(low_back(matmul_high(normed, w_qkv))).reshape(entries, pieces, 3, HEADS, head_size)
    queries = projected[:, :, 0]
    key_rows = projected[:, :, 1]
    value_rows = projected[:, :, 2]
    raw_scores = jnp.einsum('eqhd,ekhd->ehqk', queries, key_rows, precision=HIGH) * head_size ** (-0.5)
    scores = jnp.where(live_mask[:, None, None, :] > 0.5, low_back(raw_scores), MASKED)
    attention = jax.nn.softmax(scores, axis=-1)
    context = jnp.einsum('ehqk,ekhd->eqhd', low(attention), value_rows, precision=HIGH)
    context = low(low_back(context)).reshape(entries * pieces, D)
    return low(low_back(hidden + matmul_high(context, w_out) + b_out))

def ffn_half(hidden, norm_gain, w_up, b_up, w_down, b_down):
    normed = low(layer_norm(hidden, norm_gain))
    inner_act = low_back(matmul_high(normed, w_up) + b_up)
    activated = low(jax.nn.gelu(inner_act, approximate=False))
    return low(low_back(hidden + matmul_high(activated, w_down) + b_down))

def forward_block(piece_rows, live_mask, onehot, params):
    group_table, attn_gain, attn_qkv, attn_out, attn_bias, ffn_gain, ffn_up, ffn_up_bias, ffn_down, ffn_down_bias, final_gain, pool_weight, pool_bias = params
    entries = live_mask.shape[0]
    hidden = (piece_rows + matmul_high(onehot, group_table)[:, None, :]).reshape(entries * PIECES, D)
    for layer_index in range(LAYERS):
        hidden = attention_half(hidden, live_mask, attn_gain[layer_index], attn_qkv[layer_index], attn_out[layer_index], attn_bias[layer_index])
        hidden = ffn_half(hidden, ffn_gain[layer_index], ffn_up[layer_index], ffn_up_bias[layer_index], ffn_down[layer_index], ffn_down_bias[layer_index])
    pooled = low(low_back(pool_mean(hidden, live_mask, final_gain)))
    return matmul_high(pooled, pool_weight) + pool_bias

def reference(pieces, counts, groups, group_table, attn_gain, attn_qkv, attn_out, attn_bias, ffn_gain, ffn_up, ffn_up_bias, ffn_down, ffn_down_bias, final_gain, pool_weight, pool_bias, emb_cotangent):
    params = tuple((argument.astype(jnp.float32) for argument in (group_table, attn_gain, attn_qkv, attn_out, attn_bias, ffn_gain, ffn_up, ffn_up_bias, ffn_down, ffn_down_bias, final_gain, pool_weight, pool_bias)))
    blocks = N_DP
    per_block = ENTRIES // blocks

    def scan_step(totals, inputs):
        piece_blk, count_blk, group_blk, cot_blk = inputs
        live_mask = (lax.broadcasted_iota(jnp.int32, (per_block, PIECES), 1) < count_blk[:, None]).astype(jnp.float32)
        onehot = (group_blk[:, None] == lax.broadcasted_iota(jnp.int32, (per_block, GROUPS), 1)).astype(jnp.float32)

        def run_block(piece_in, *weights):
            return forward_block(piece_in, live_mask, onehot, weights)
        embedded, pullback = jax.vjp(run_block, piece_blk.astype(jnp.float32), *params)
        gradients = pullback(cot_blk.astype(jnp.float32))
        totals = tuple((running + addend for running, addend in zip(totals, gradients[1:])))
        return (totals, (embedded.astype(jnp.bfloat16), gradients[0].astype(jnp.bfloat16)))
    zeros = tuple((jnp.zeros_like(argument) for argument in params))
    sums, (embedded, piece_grads) = lax.scan(scan_step, zeros, (pieces.reshape(blocks, per_block, PIECES, D), counts.reshape(blocks, per_block), groups.reshape(blocks, per_block), emb_cotangent.reshape(blocks, per_block, PROJ)))
    table_grad, attn_gain_grad, attn_qkv_grad, attn_out_grad, attn_bias_grad, ffn_gain_grad, ffn_up_grad, ffn_up_bias_grad, ffn_down_grad, ffn_down_bias_grad, final_gain_grad, pool_weight_grad, pool_bias_grad = sums
    return (embedded.reshape(ENTRIES, PROJ), piece_grads.reshape(ENTRIES, PIECES, D), table_grad, attn_gain_grad, attn_qkv_grad, attn_out_grad, attn_bias_grad, ffn_gain_grad, ffn_up_grad, ffn_up_bias_grad, ffn_down_grad, ffn_down_bias_grad, final_gain_grad, pool_weight_grad, pool_bias_grad)
```

```python
import jax
import jax.numpy as jnp
from jax import lax
from jax.sharding import PartitionSpec as P

HEADS = 8


EPS = 1e-05
MASKED = -1e30
HIGH = lax.Precision.HIGHEST


def layer_norm(values, norm_gain):
    centre = values - jnp.mean(values, axis=-1, keepdims=True)
    spread = jnp.mean(centre * centre, axis=-1, keepdims=True)
    return centre * lax.rsqrt(spread + EPS) * norm_gain


def pool_mean(hidden, live_mask, norm_gain):
    entries, pieces = live_mask.shape
    normed = layer_norm(hidden, norm_gain).reshape(entries, pieces, -1)
    return jnp.sum(normed * live_mask[:, :, None], axis=1) / jnp.sum(
        live_mask, axis=1, keepdims=True
    )


def matmul_plain(left_side, right_side):
    return jnp.dot(left_side, right_side, preferred_element_type=jnp.float32)


def matmul_left(left_side, right_side):
    return lax.dot_general(
        left_side, right_side, (((0,), (0,)), ((), ())), preferred_element_type=jnp.float32
    )


def matmul_right(left_side, right_side):
    return lax.dot_general(
        left_side, right_side, (((1,), (1,)), ((), ())), preferred_element_type=jnp.float32
    )


def gelu_exact(values):
    return jax.nn.gelu(values, approximate=False)


def attend_forward(hidden, live_mask, weights):
    norm_gain, w_qkv, w_out, b_out = weights
    entries, pieces = live_mask.shape
    model_width = hidden.shape[1]
    head_size = model_width // HEADS
    normed, norm_back = jax.vjp(layer_norm, hidden, norm_gain)
    normed_low = normed.astype(jnp.bfloat16)
    projected = matmul_plain(normed_low, w_qkv).astype(jnp.bfloat16)
    projected = projected.reshape(entries, pieces, 3, HEADS, head_size)
    queries = projected[:, :, 0]
    key_rows = projected[:, :, 1]
    value_rows = projected[:, :, 2]
    scores = jnp.einsum(
        "eqhd,ekhd->ehqk", queries, key_rows, preferred_element_type=jnp.float32
    ) * head_size ** (-0.5)
    scores = jnp.where(live_mask[:, None, None, :] > 0.5, scores, MASKED)
    shifted = jnp.exp(scores - jnp.max(scores, axis=-1, keepdims=True))
    attention = shifted / jnp.sum(shifted, axis=-1, keepdims=True)
    attention_low = attention.astype(jnp.bfloat16)
    context = jnp.einsum(
        "ehqk,ekhd->eqhd", attention_low, value_rows, preferred_element_type=jnp.float32
    )
    context = context.astype(jnp.bfloat16).reshape(entries * pieces, model_width)
    section_out = (hidden + matmul_plain(context, w_out) + b_out).astype(jnp.bfloat16)
    saved_state = (
        norm_back,
        normed_low,
        queries,
        key_rows,
        value_rows,
        attention,
        attention_low,
        context,
    )
    return (section_out, saved_state)


def attend_backward(saved_state, grad_low, live_mask, weights, grad_acc):
    norm_gain, w_qkv, w_out, b_out = weights
    entries, pieces = live_mask.shape
    model_width = w_out.shape[0]
    head_size = model_width // HEADS
    norm_back, normed_low, queries, key_rows, value_rows, attention, attention_low, context = (
        saved_state
    )
    gain_sum, qkv_sum, out_sum, bias_sum = grad_acc
    grad_wide = grad_low.astype(jnp.float32)
    out_sum = out_sum + matmul_left(context, grad_low)
    bias_sum = bias_sum + jnp.sum(grad_wide, axis=0)
    d_context = (
        matmul_right(grad_low, w_out)
        .astype(jnp.bfloat16)
        .reshape(entries, pieces, HEADS, head_size)
    )
    d_attention = jnp.einsum(
        "eqhd,ekhd->ehqk", d_context, value_rows, preferred_element_type=jnp.float32
    )
    d_values = jnp.einsum(
        "ehqk,eqhd->ekhd", attention_low, d_context, preferred_element_type=jnp.float32
    )
    d_scores = attention * (d_attention - jnp.sum(attention * d_attention, axis=-1, keepdims=True))
    d_scores = d_scores.astype(jnp.bfloat16)
    d_queries = jnp.einsum(
        "ehqk,ekhd->eqhd", d_scores, key_rows, preferred_element_type=jnp.float32
    ) * head_size ** (-0.5)
    d_keys = jnp.einsum(
        "ehqk,eqhd->ekhd", d_scores, queries, preferred_element_type=jnp.float32
    ) * head_size ** (-0.5)
    d_projected = jnp.stack([d_queries, d_keys, d_values], axis=2).astype(jnp.bfloat16)
    d_projected = d_projected.reshape(entries * pieces, 3 * model_width)
    qkv_sum = qkv_sum + matmul_left(normed_low, d_projected)
    d_hidden, gain_term = norm_back(matmul_right(d_projected, w_qkv))
    return (d_hidden + grad_wide, (gain_sum + gain_term, qkv_sum, out_sum, bias_sum))


def feed_forward(hidden, weights):
    norm_gain, w_up, b_up, w_down, b_down = weights
    normed, norm_back = jax.vjp(layer_norm, hidden, norm_gain)
    normed_low = normed.astype(jnp.bfloat16)
    inner_act = matmul_plain(normed_low, w_up) + b_up
    activated, gelu_back = jax.vjp(gelu_exact, inner_act)
    activated_low = activated.astype(jnp.bfloat16)
    section_out = (hidden + matmul_plain(activated_low, w_down) + b_down).astype(jnp.bfloat16)
    return (section_out, (norm_back, normed_low, gelu_back, activated_low))


def feed_backward(grad_low, saved_state, weights, grad_acc):
    norm_gain, w_up, b_up, w_down, b_down = weights
    norm_back, normed_low, gelu_back, activated_low = saved_state
    gain_sum, up_sum, up_bias_sum, down_sum, down_bias_sum = grad_acc
    grad_wide = grad_low.astype(jnp.float32)
    down_sum = down_sum + matmul_left(activated_low, grad_low)
    down_bias_sum = down_bias_sum + jnp.sum(grad_wide, axis=0)
    d_inner = gelu_back(matmul_right(grad_low, w_down))[0].astype(jnp.bfloat16)
    up_sum = up_sum + matmul_left(normed_low, d_inner)
    up_bias_sum = up_bias_sum + jnp.sum(d_inner.astype(jnp.float32), axis=0)
    d_hidden, gain_term = norm_back(matmul_right(d_inner, w_up))
    return (
        d_hidden + grad_wide,
        (gain_sum + gain_term, up_sum, up_bias_sum, down_sum, down_bias_sum),
    )


def per_device(
    pieces,
    counts,
    groups,
    group_table,
    attn_gain,
    attn_qkv,
    attn_out,
    attn_bias,
    ffn_gain,
    ffn_up,
    ffn_up_bias,
    ffn_down,
    ffn_down_bias,
    final_gain,
    pool_weight,
    pool_bias,
    emb_cotangent,
):
    entries, pieces_max, model_width = pieces.shape
    token_rows = entries * pieces_max
    group_count = group_table.shape[0]
    layer_count = attn_qkv.shape[0]
    wide = lambda a: a.astype(jnp.float32)
    live_mask = wide(lax.broadcasted_iota(jnp.int32, (entries, pieces_max), 1) < counts[:, None])
    onehot = wide(groups[:, None] == lax.broadcasted_iota(jnp.int32, (entries, group_count), 1))
    group_rows = matmul_plain(onehot.astype(jnp.bfloat16), group_table)
    hidden = (wide(pieces) + group_rows[:, None, :]).reshape(token_rows, model_width)
    saved = []
    for layer in range(layer_count):
        attn_weights = (wide(attn_gain[layer]), attn_qkv[layer], attn_out[layer], wide(attn_bias[layer]))
        ffn_weights = (
            wide(ffn_gain[layer]),
            ffn_up[layer],
            wide(ffn_up_bias[layer]),
            ffn_down[layer],
            wide(ffn_down_bias[layer]),
        )
        middle, attn_state = attend_forward(hidden, live_mask, attn_weights)
        after, ffn_state = feed_forward(wide(middle), ffn_weights)
        saved.append((hidden, attn_state, attn_weights, ffn_state, ffn_weights))
        hidden = wide(after)
    pooled_wide, pool_back = jax.vjp(
        lambda values, gain: pool_mean(values, live_mask, gain), hidden, wide(final_gain)
    )
    pooled = pooled_wide.astype(jnp.bfloat16)
    embeddings = (matmul_plain(pooled, pool_weight) + wide(pool_bias)).astype(jnp.bfloat16)
    pool_term = matmul_left(pooled, emb_cotangent)
    pool_bias_term = jnp.sum(wide(emb_cotangent), axis=0)
    d_pooled = matmul_right(emb_cotangent, pool_weight).astype(jnp.bfloat16)
    d_hidden, end_term = pool_back(wide(d_pooled))

    def reduced(term, dim):
        part = lax.psum_scatter(term.astype(jnp.bfloat16), "dp", scatter_dimension=dim, tiled=True)
        return wide(lax.psum(part, "section"))

    layer_terms = [None] * layer_count
    for layer in reversed(range(layer_count)):
        hidden_in, attn_state, attn_weights, ffn_state, ffn_weights = saved[layer]
        zeros5 = (0.0,) * 5
        d_hidden, ffn_terms = feed_backward(
            d_hidden.astype(jnp.bfloat16), ffn_state, ffn_weights, zeros5
        )
        d_hidden, attn_terms = attend_backward(
            attn_state, d_hidden.astype(jnp.bfloat16), live_mask, attn_weights, (0.0,) * 4
        )
        layer_terms[layer] = tuple(attn_terms) + tuple(ffn_terms)
    input_grad = d_hidden.astype(jnp.bfloat16).reshape(entries, pieces_max, model_width)
    piece_sums = jnp.sum(d_hidden.reshape(entries, pieces_max, model_width), axis=1)
    table_term = lax.dot_general(
        onehot, piece_sums, (((0,), (0,)), ((), ())), precision=HIGH, preferred_element_type=jnp.float32
    )
    stacked = [jnp.stack([terms[k] for terms in layer_terms]) for k in range(9)]
    totals = [reduced(term, 1) for term in stacked]
    return (
        embeddings,
        input_grad,
        reduced(table_term, 1),
        *totals,
        reduced(end_term, 0),
        reduced(pool_term, 0),
        reduced(pool_bias_term, 0),
    )


def solution(mesh):
    placed = (
        P(("dp", "section"), None, None),
        P(("dp", "section")),
        P(("dp", "section")),
        P(),
        P(),
        P(),
        P(),
        P(),
        P(),
        P(),
        P(),
        P(),
        P(),
        P(),
        P(),
        P(),
        P(("dp", "section"), None),
    )
    return jax.shard_map(
        per_device,
        mesh=mesh,
        in_specs=placed,
        out_specs=(
            P(("dp", "section"), None),
            P(("dp", "section"), None, None),
            P(None, "dp"),
            P(None, "dp"),
            P(None, "dp", None),
            P(None, "dp", None),
            P(None, "dp"),
            P(None, "dp"),
            P(None, "dp", None),
            P(None, "dp"),
            P(None, "dp", None),
            P(None, "dp"),
            P("dp"),
            P("dp", None),
            P("dp"),
        ),
        check_vma=False,
    )
```

```python
import functools

import jax
import jax.numpy as jnp
from jax import lax
from jax.experimental import pallas as pl
from jax.experimental.pallas import tpu as pltpu
from jax.sharding import PartitionSpec as P

HEADS = 8
EPS = 1e-05
MASKED = -1e30
F32 = jnp.float32
BF16 = jnp.bfloat16
MESH = pl.DeviceIdType.MESH
SHARDS = 8
PIECE = 16
GROUPS_OUT = 7
SLOTS = 3


def mm(left, right):
    return jnp.dot(left, right, preferred_element_type=F32)


def mm_right(left, right):
    return lax.dot_general(left, right, (((1,), (1,)), ((), ())), preferred_element_type=F32)


def flipped(value, mask):
    return value + mask - 2 * mask * ((value // mask) % 2)


def normalised(values):
    centre = values - jnp.mean(values, axis=-1, keepdims=True)
    scale = lax.rsqrt(jnp.mean(centre * centre, axis=-1, keepdims=True) + EPS)
    return centre * scale, scale


def gelu_both(v):
    size = jnp.abs(v)
    t = 1.0 / (1.0 + (0.3275911 * 0.7071067811865476) * size)
    bell = jnp.exp(-0.5 * (v * v))
    poly = t * (
        0.127414796
        + t * (-0.142248368 + t * (0.7107068705 + t * (-0.7265760135 + t * 0.5307027145)))
    )
    tail = poly * bell
    cdf = jnp.where(v >= 0, 1.0 - tail, tail)
    return v * cdf, cdf + v * (bell * 0.3989422804014327)


PARTS = {
    "a": (slice(0, 2), ("x", "y", "zl", "zh")),
    "b": (slice(2, 3), ("y", "x", "zl", "zh")),
    "c": (slice(3, 4), ("zl", "zh", "x", "y")),
}
AXES = ("y", "zh", "zl", "x")


def kernel(rem, plan, *refs):
    (
        pieces_ref, counts_ref, groups_ref, table_ref, again_ref, abias_ref, fgain_ref, ubias_ref, dbias_ref,
        egain_ref, pbias_ref, cot_ref, wqkv_hbm, wout_hbm, wup_hbm, wdown_hbm, wpool_hbm,
        emb_ref, dx_ref, fin_ref, small_ref,
        wqkv, wout, wup, wdown, wpool, es, ex, x3, x0, hs, nb, qkv, prob, ctx, act, dg, dyw, dyb, dqkv, wide, tmp, npool, upool,
        g_buf, r0, ra, rb, rc, f_buf, s_buf, w_sem, send_sem, recv_sem, sm_send, sm_recv, out_sem,
    ) = refs
    entries, slots, width = pieces_ref.shape
    layers = again_ref.shape[0]
    token_rows = slots * entries
    b = lax.axis_index("dp") // rem
    s = lax.axis_index("section")
    bits = {"zh": b // 4, "zl": (b // 2) % 2, "x": b % 2, "y": s // 2, "core": s % 2}
    dp_mask = {"zh": 4 * rem, "zl": 2 * rem, "x": rem, "y": 0, "core": 0}
    sec_mask = {"zh": 0, "zl": 0, "x": 0, "y": 2, "core": 1}

    def partner(axis):
        d, e = lax.axis_index("dp"), lax.axis_index("section")
        return (
            flipped(d, dp_mask[axis]) if dp_mask[axis] else d,
            flipped(e, sec_mask[axis]) if sec_mask[axis] else e,
        )

    barrier = pltpu.get_barrier_semaphore()
    for axis in bits:
        pl.semaphore_signal(barrier, inc=1, device_id=partner(axis), device_id_type=MESH)

    loads = {}
    order = []
    for layer in range(layers):
        order += [("qkv", layer, wqkv_hbm, wqkv), ("out", layer, wout_hbm, wout), ("up", layer, wup_hbm, wup), ("down", layer, wdown_hbm, wdown)]
    for at, (name, layer, source, target) in enumerate(order):
        loads[name, layer] = pltpu.make_async_copy(source.at[layer], target.at[layer], w_sem.at[at])
        loads[name, layer].start()
    loads["pool", 0] = pltpu.make_async_copy(wpool_hbm, wpool, w_sem.at[len(order)])
    loads["pool", 0].start()

    def rows(j):
        return pl.ds(pl.multiple_of(j * entries, entries), entries)

    def column(row_ref):
        eye = lax.broadcasted_iota(jnp.int32, (entries, entries), 0) == lax.broadcasted_iota(
            jnp.int32, (entries, entries), 1
        )
        row = row_ref[...].astype(F32)
        return jnp.sum(jnp.where(eye, row, 0.0), axis=1, keepdims=True)

    count = column(counts_ref)
    group = column(groups_ref)

    head_of = lax.broadcasted_iota(jnp.int32, (width, 128), 0) // (width // HEADS)
    lane_of = lax.broadcasted_iota(jnp.int32, (width, 128), 1) % 64
    head_of_t = lax.broadcasted_iota(jnp.int32, (128, width), 1) // (width // HEADS)
    lane_of_t = lax.broadcasted_iota(jnp.int32, (128, width), 0)
    scaling = (width // HEADS) ** -0.5
    for j in range(slots):
        es[j] = jnp.where(lane_of - head_of == j * HEADS, scaling, 0.0).astype(BF16)
        ex[j] = jnp.where(lane_of_t - head_of_t == j * HEADS, 1.0, 0.0).astype(BF16)
    live_lanes = (
        (lax.broadcasted_iota(jnp.int32, (entries, 128), 1) % 64) // HEADS
    ).astype(F32) < count

    x3[:, 0:slots, :] = pieces_ref[...].astype(F32)
    group_rows = jnp.zeros((entries, width), F32)
    for g in range(table_ref.shape[0]):
        group_rows = jnp.where(group == g, table_ref[g : g + 1, :].astype(F32), group_rows)
    for j in range(slots):
        x0[j * entries : (j + 1) * entries, :] = x3[:, j, :] + group_rows

    def norm_rows(source, gain):
        @pl.loop(0, slots)
        def _(j):
            n, _r = normalised(source[rows(j), :].astype(F32))
            nb[rows(j), :] = (n * gain).astype(BF16)

    def rolled(value, op):
        for shift in (8, 16, 32):
            value = op(value, pltpu.roll(value, shift, 1))
        return value

    def spread_rows(block, value):
        n = value.shape[-1]
        return (value.reshape(slots, entries, n) * block[None]).reshape(token_rows, n)

    def attention_forward(layer, source, target):
        norm_rows(source, again_ref[layer : layer + 1, :].astype(F32))
        loads["qkv", layer].wait()
        for t in range(3):
            cols = pl.ds(t * width, width)
            qkv[layer, :, cols] = mm(nb[...], wqkv[layer, :, cols]).astype(BF16)
        scores = jnp.zeros((token_rows, 128), F32)
        for j in range(slots):
            k = qkv[layer, rows(j), width : 2 * width]
            scores += mm(spread_rows(k, qkv[layer, :, 0:width]), es[j])
        scores = jnp.where(live_lanes[None], scores.reshape(slots, entries, 128), MASKED).reshape(token_rows, 128)
        raised = jnp.exp(scores - rolled(scores, jnp.maximum))
        p = raised / rolled(raised, jnp.add)
        prob[layer] = p
        p_low = p.astype(BF16)

        @pl.loop(0, width // 128)
        def _(c):
            lanes = pl.ds(pl.multiple_of(c * 128, 128), 128)
            v_lanes = pl.ds(pl.multiple_of(2 * width + c * 128, 128), 128)
            total = jnp.zeros((token_rows, 128), F32)
            for j in range(slots):
                total += spread_rows(qkv[layer, rows(j), v_lanes].astype(F32), mm(p_low, ex[j, :, lanes]))
            ctx[layer, :, lanes] = total.astype(BF16)

        loads["out", layer].wait()
        bias = abias_ref[layer : layer + 1, :].astype(F32)
        hs[target] = (source[...].astype(F32) + mm(ctx[layer], wout[layer]) + bias).astype(BF16)

    def ffn_forward(layer, source, target):
        norm_rows(source, fgain_ref[layer : layer + 1, :].astype(F32))
        loads["up", layer].wait()

        @pl.loop(0, wup.shape[2] // 256)
        def _(t):
            cols = pl.ds(pl.multiple_of(t * 256, 256), 256)
            inner = mm(nb[...], wup[layer, :, cols]) + ubias_ref[layer : layer + 1, cols].astype(F32)
            activated, slope = gelu_both(inner)
            act[layer, :, cols] = activated.astype(BF16)
            dg[layer, :, cols] = slope.astype(BF16)

        loads["down", layer].wait()
        bias = dbias_ref[layer : layer + 1, :].astype(F32)
        hs[target] = (source[...].astype(F32) + mm(act[layer], wdown[layer]) + bias).astype(BF16)

    def put_columns(slot, quantum, value):
        block = value.astype(BF16)
        for o in range(SHARDS):
            for y in range(2):
                for c in range(2):
                    at = o * 64 + y * 32 + c * PIECE
                    g_buf[slot, quantum, c, y, o // 4, (o // 2) % 2, o % 2] = block[at : at + PIECE]

    def put_down(slot, t, value):
        block = value.astype(BF16)
        for half in range(2):
            for k in range(4):
                for y in range(2):
                    for c in range(2):
                        at = half * 256 + k * 64 + y * 32 + c * PIECE
                        g_buf[slot, k, c, y, t // 2, t % 2, half] = block[at : at + PIECE]

    def col_sum(value):
        return jnp.sum(value, axis=0, keepdims=True)

    def own(view, lead, axis_list, axis, index, full=None):
        spots = [slice(None)] * lead + [index if a == axis else slice(None) for a in axis_list]
        return view.at[tuple(spots)]

    part_buffers = {"a": ra, "b": rb, "c": rc}

    def stage_views(g, part, stage):
        quanta, dims = PARTS[part]
        count_q = quanta.stop - quanta.start
        if stage == 0:
            slot = g % SLOTS
            core = bits["core"]
            source = g_buf.at[slot, quanta, 1 - core]
            mine = g_buf.at[slot, quanta, core]
            return "core", source, mine, r0.at[g, quanta]
        if stage <= 4:
            axis = dims[stage - 1]
            left = [a for a in AXES if a not in dims[: stage - 1]]
            before = r0.at[g, quanta] if stage == 1 else part_buffers[part][stage - 2].at[g]
            after = part_buffers[part][stage - 1].at[g]
            spots = [slice(None)] + [slice(None)] * len(left)
            spots[1 + left.index(axis)] = 1 - bits[axis]
            source = before.at[tuple(spots)]
            spots[1 + left.index(axis)] = bits[axis]
            return axis, source, before.at[tuple(spots)], after
        y, core = bits["y"], bits["core"]
        if stage == 5:
            view = f_buf.at[g, quanta, y, core]
            return "y", view, None, view
        view = f_buf.at[g, quanta, :, core]
        return "core", view, None, view

    part_at = {"a": 0, "b": 1, "c": 2}

    def copy_of(g, part, stage):
        axis, source, mine, landing = stage_views(g, part, stage)
        at = part_at[part]
        return pltpu.make_async_remote_copy(
            src_ref=source,
            dst_ref=landing,
            send_sem=send_sem.at[g, at, stage],
            recv_sem=recv_sem.at[g, at, stage],
            device_id=partner(axis),
            device_id_type=MESH,
        )

    def start(g, part, stage):
        copy_of(g, part, stage).start()

    def finish(g, part, stage):
        axis, source, mine, landing = stage_views(g, part, stage)
        copy_of(g, part, stage).wait()
        if stage < 4:
            landing[...] = landing[...] + mine[...]
        elif stage == 4:
            quanta = PARTS[part][0]
            f_buf[g, quanta, bits["y"], bits["core"]] = landing[...] + mine[...]

    def advance(g, part, stage):
        if stage >= 0:
            finish(g, part, stage)
        if stage < 6:
            start(g, part, stage + 1)

    def small_copy(stage):
        axis = ("core", "x", "y", "zl", "zh")[stage]
        return pltpu.make_async_remote_copy(
            src_ref=s_buf.at[2 * stage],
            dst_ref=s_buf.at[2 * stage + 1],
            send_sem=sm_send.at[stage],
            recv_sem=sm_recv.at[stage],
            device_id=partner(axis),
            device_id_type=MESH,
        )

    def small(stage):
        if stage >= 0:
            small_copy(stage).wait()
            s_buf[2 * stage + 2] = s_buf[2 * stage] + s_buf[2 * stage + 1]
        if stage < 4:
            small_copy(stage + 1).start()

    def put_small(at, value):
        s_buf[0, pl.ds(at, value.shape[0]), :] = value

    def forward():
        for layer in range(layers):
            attention_forward(layer, x0 if layer == 0 else hs.at[2 * layer - 1], 2 * layer)
            ffn_forward(layer, hs.at[2 * layer], 2 * layer + 1)

        live_sum = jnp.zeros((entries, width), F32)
        for j in range(slots):
            n, _r = normalised(hs[2 * layers - 1, rows(j), :].astype(F32))
            live_sum += jnp.where(count > j, n, 0.0)
        npool[...] = live_sum / count
        pooled = (npool[...] * egain_ref[...].astype(F32)).astype(BF16)
        pooled_t = pooled.astype(F32).T.astype(BF16)
        loads["pool", 0].wait()
        for k in range(4):
            put_columns(0, k, mm(pooled_t, cot_ref[:, k * width : (k + 1) * width]))

    def embed():
        pooled = (npool[...] * egain_ref[...].astype(F32)).astype(BF16)
        for k in range(4):
            cols = slice(k * width, (k + 1) * width)
            emb_ref[:, cols] = (mm(pooled, wpool[:, cols]) + pbias_ref[:, cols].astype(F32)).astype(BF16)

    def pool_backward():
        for k in range(4):
            put_small(17 + k, col_sum(cot_ref[:, k * width : (k + 1) * width].astype(F32)))
        d_pooled = mm_right(cot_ref[...], wpool[...]).astype(BF16).astype(F32)
        put_small(16, col_sum(d_pooled * npool[...]))
        upool[...] = d_pooled * egain_ref[...].astype(F32) / count
        for j in range(slots):
            n, r = normalised(hs[2 * layers - 1, rows(j), :].astype(F32))
            u = jnp.where(count > j, upool[...], 0.0)
            d = r * (u - jnp.mean(u, axis=-1, keepdims=True) - n * jnp.mean(u * n, axis=-1, keepdims=True))
            dyb[rows(j), :] = d.astype(BF16)

    def norm_backward(source, gain, at, keep_wide):
        def step(j, total):
            n, r = normalised(source[rows(j), :].astype(F32))
            d_normed = wide[rows(j), :]
            u = d_normed * gain
            d = r * (u - jnp.mean(u, axis=-1, keepdims=True) - n * jnp.mean(u * n, axis=-1, keepdims=True))
            d_h = dyb[rows(j), :].astype(F32) + d
            dyb[rows(j), :] = d_h.astype(BF16)
            if keep_wide:
                wide[rows(j), :] = d_h
            return total + d_normed * n

        total = lax.fori_loop(0, slots, step, jnp.zeros((entries, width), F32))
        put_small(at, col_sum(total))

    def dy_sum(at):
        put_small(at, col_sum(dyb[...].astype(F32)))

    def turned(value):
        return value.astype(F32).T.astype(BF16)

    def down_grad(layer, slot):
        dy_sum(8 * layer + 3)

        @pl.loop(0, 4)
        def _(t):
            cols = pl.ds(pl.multiple_of(t * width, width), width)
            put_down(slot, t, mm(turned(act[layer, :, cols]), dyb[...]))

    def up_grad(layer, slot, source):
        gain = fgain_ref[layer : layer + 1, :].astype(F32)
        norm_rows(source, gain)
        tmp[...] = turned(nb[...])

        @pl.loop(0, 4)
        def _(t):
            cols = pl.ds(pl.multiple_of(t * width, width), width)
            d_act = mm_right(dyb[...], wdown[layer, cols, :])
            d_inner = (d_act * dg[layer, :, cols].astype(F32)).astype(BF16)
            put_small(8 * layer + 4 + t, col_sum(d_inner.astype(F32)))
            put_columns(slot, t, mm(tmp[...], d_inner))
            dqkv[:, cols] = d_inner

        wide[...] = mm_right(dqkv[...], wup[layer])
        norm_backward(source, gain, 8 * layer + 2, False)

    def attention_grad(layer, slot, source):
        gain = again_ref[layer : layer + 1, :].astype(F32)
        dy_sum(8 * layer + 1)
        put_columns(slot, 3, mm(turned(ctx[layer]), dyb[...]))
        nb[...] = mm_right(dyb[...], wout[layer]).astype(BF16)
        d_prob = jnp.zeros((token_rows, 128), F32)
        for j in range(slots):
            v = qkv[layer, rows(j), 2 * width : 3 * width]
            d_prob += mm(spread_rows(v, nb[...]), es[j])
        d_prob = d_prob * (1.0 / scaling)
        p = prob[layer]
        p_low = p.astype(BF16)
        mixed = p * d_prob
        d_scores = (mixed - p * rolled(mixed, jnp.add)).astype(BF16)

        @pl.loop(0, width // 128)
        def _(c):
            def lanes(part):
                return pl.ds(pl.multiple_of(part * width + c * 128, 128), 128)

            d_q = jnp.zeros((token_rows, 128), F32)
            for j in range(slots):
                weights = mm(p_low, ex[j, :, lanes(0)])
                d_v = jnp.sum((weights * nb[:, lanes(0)].astype(F32)).reshape(slots, entries, 128), axis=0)
                weights = mm(d_scores, ex[j, :, lanes(0)])
                d_q += spread_rows(qkv[layer, rows(j), lanes(1)].astype(F32), weights)
                d_k = jnp.sum((weights * qkv[layer, :, lanes(0)].astype(F32)).reshape(slots, entries, 128), axis=0)
                dqkv[rows(j), lanes(1)] = (d_k * scaling).astype(BF16)
                dqkv[rows(j), lanes(2)] = d_v.astype(BF16)
            dqkv[:, lanes(0)] = (d_q * scaling).astype(BF16)

        norm_rows(source, gain)
        tmp[...] = turned(nb[...])
        for t in range(3):
            put_columns(slot, t, mm(tmp[...], dqkv[:, t * width : (t + 1) * width]))
        wide[...] = mm_right(dqkv[:, 0 : 3 * width], wqkv[layer])
        norm_backward(source, gain, 8 * layer, layer == 0)

    def finish_input():
        sums = jnp.zeros((entries, width), F32)
        for j in range(slots):
            sums += wide[j * entries : (j + 1) * entries, :]
            x3[:, j, :] = wide[j * entries : (j + 1) * entries, :]
        dx_ref[...] = x3[:, 0:slots, :].astype(BF16)
        for g in range(table_ref.shape[0]):
            put_small(24 + g, col_sum(jnp.where(group == g, sums, 0.0)))

    s_buf[0] = jnp.zeros(s_buf.shape[1:], F32)

    computations = {
        "forward": forward,
        "embed": embed,
        "pool_backward": pool_backward,
        "down1": lambda: down_grad(1, 1 % SLOTS),
        "up1": lambda: up_grad(1, 2 % SLOTS, hs.at[2]),
        "attn1": lambda: attention_grad(1, 3 % SLOTS, hs.at[1]),
        "down0": lambda: down_grad(0, 4 % SLOTS),
        "up0": lambda: up_grad(0, 5 % SLOTS, hs.at[0]),
        "attn0": lambda: attention_grad(0, 6 % SLOTS, x0),
        "input": finish_input,
    }
    entered = False
    for item in plan:
        if item[0] == "compute":
            computations[item[1]]()
            continue
        if not entered:
            pl.semaphore_wait(barrier, 5)
            entered = True
        if item[0] == "advance":
            advance(*item[1:])
        elif item[0] == "small":
            small(item[1])
    done = pltpu.make_async_copy(f_buf, fin_ref, out_sem)
    done.start()
    small_ref[...] = s_buf[10]
    done.wait()


def plan_of():
    names = ["forward", "down1", "up1", "attn1", "down0", "up0", "attn0"]
    plan = []
    for tick in range(GROUPS_OUT + 7):
        if tick < GROUPS_OUT:
            plan.append(("compute", names[tick]))
            for part in PARTS:
                plan.append(("advance", tick, part, -1))
        if tick == 0:
            plan.append(("compute", "pool_backward"))
        if tick == 1:
            plan.append(("compute", "embed"))
        if tick == 6:
            plan.append(("compute", "input"))
            plan.append(("small", -1))
        if tick > 6 and tick < 12:
            plan.append(("small", tick - 7))
        for g in range(GROUPS_OUT):
            stage = tick - 1 - g
            if 0 <= stage <= 6:
                for part in PARTS:
                    plan.append(("advance", g, part, stage))
    return tuple(plan)


def per_device(rem, plan, pieces, counts, groups, table, again, wqkv, wout, abias, fgain, wup, ubias, wdown, dbias, egain, wpool, pbias, cot):
    entries, slots, width = pieces.shape
    hidden = wup.shape[2]
    layers = wqkv.shape[0]
    token_rows = entries * slots
    vmem = pl.BlockSpec(memory_space=pltpu.VMEM)
    hbm = pl.BlockSpec(memory_space=pl.ANY)
    tile = (PIECE, width)

    def buffers(part):
        quanta, dims = PARTS[part]
        size = quanta.stop - quanta.start
        return [pltpu.VMEM((GROUPS_OUT, size) + (2,) * (3 - k) + tile, BF16) for k in range(4)]

    def body(*refs):
        refs = list(refs)
        fixed = 17 + 4 + 25
        head, rest = refs[: fixed], refs[fixed:]
        parts = [rest[4 * k : 4 * k + 4] for k in range(3)]
        kernel(rem, plan, *head, *parts, *rest[12:])

    scratch = [
        pltpu.VMEM(wqkv.shape, BF16), pltpu.VMEM(wout.shape, BF16), pltpu.VMEM(wup.shape, BF16), pltpu.VMEM(wdown.shape, BF16),
        pltpu.VMEM(wpool.shape, BF16), pltpu.VMEM((slots, width, 128), BF16), pltpu.VMEM((slots, 128, width), BF16),
        pltpu.VMEM((entries, 8, width), F32), pltpu.VMEM((token_rows, width), F32), pltpu.VMEM((2 * layers, token_rows, width), BF16),
        pltpu.VMEM((token_rows, width), BF16), pltpu.VMEM((layers, token_rows, 3 * width), BF16), pltpu.VMEM((layers, token_rows, 128), F32),
        pltpu.VMEM((layers, token_rows, width), BF16), pltpu.VMEM((layers, token_rows, hidden), BF16), pltpu.VMEM((layers, token_rows, hidden), BF16),
        pltpu.VMEM((8, 128), F32), pltpu.VMEM((token_rows, width), BF16), pltpu.VMEM((token_rows, hidden), BF16), pltpu.VMEM((token_rows, width), F32),
        pltpu.VMEM((width, token_rows), BF16), pltpu.VMEM((entries, width), F32), pltpu.VMEM((entries, width), F32),
        pltpu.VMEM((SLOTS, 4, 2, 2, 2, 2, 2) + tile, BF16), pltpu.VMEM((GROUPS_OUT, 4, 2, 2, 2, 2) + tile, BF16),
        *buffers("a"), *buffers("b"), *buffers("c"),
        pltpu.VMEM((GROUPS_OUT, 4, 2, 2) + tile, BF16), pltpu.VMEM((11, 32, width), F32),
        pltpu.SemaphoreType.DMA((4 * layers + 1,)), pltpu.SemaphoreType.DMA((GROUPS_OUT, 3, 7)), pltpu.SemaphoreType.DMA((GROUPS_OUT, 3, 7)),
        pltpu.SemaphoreType.DMA((5,)), pltpu.SemaphoreType.DMA((5,)), pltpu.SemaphoreType.DMA,
    ]
    emb, dx, fin, small = pl.pallas_call(
        body,
        out_shape=(
            jax.ShapeDtypeStruct((entries, wpool.shape[1]), BF16),
            jax.ShapeDtypeStruct(pieces.shape, BF16),
            jax.ShapeDtypeStruct((GROUPS_OUT, 4, 2, 2) + tile, BF16),
            jax.ShapeDtypeStruct((32, width), F32),
        ),
        in_specs=[vmem] * 12 + [hbm] * 5,
        out_specs=(vmem, vmem, hbm, vmem),
        scratch_shapes=scratch,
        compiler_params=pltpu.CompilerParams(collective_id=0, has_side_effects=True, vmem_limit_bytes=64 * 2**20),
    )(
        pieces, counts.reshape(1, -1), groups.reshape(1, -1), table, again, abias, fgain, ubias, dbias,
        egain.reshape(1, -1), pbias.reshape(1, -1), cot, wqkv, wout, wup, wdown, wpool,
    )
    return emb, dx, fin, small


def unpack(rem, emb, dx, fin, small):
    wide = fin.reshape(GROUPS_OUT, 4, 64, fin.shape[-1]).astype(F32)

    def columns(group, lo, hi):
        return jnp.concatenate([wide[group, k] for k in range(lo, hi)], axis=-1)

    down = jnp.stack([wide[4].reshape(256, -1), wide[1].reshape(256, -1)])
    up = jnp.stack([columns(5, 0, 4), columns(2, 0, 4)])
    out = jnp.stack([wide[6, 3], wide[3, 3]])
    qkv = jnp.stack([columns(6, 0, 3), columns(3, 0, 3)])
    pool = columns(0, 0, 4)
    part = lax.axis_index("dp") // rem

    def share(value):
        return lax.dynamic_slice_in_dim(value, part * (value.shape[-1] // SHARDS), value.shape[-1] // SHARDS, value.ndim - 1)

    layered = [share(jnp.stack([small[k], small[8 + k]])) for k in range(4)]
    ubias = share(jnp.stack([small[4:8].reshape(-1), small[12:16].reshape(-1)]))
    grads = [
        (share(small[24:32]), 1), (layered[0], 1), (qkv, 1), (out, 1), (layered[1], 1), (layered[2], 1), (up, 1), (ubias, 1),
        (down, 1), (layered[3], 1), (share(small[16]), 0), (pool, 0), (share(small[17:21].reshape(-1)), 0),
    ]
    if rem > 1:
        blocks = [list(range(k * rem, (k + 1) * rem)) for k in range(SHARDS)]
        grads = [
            (lax.psum_scatter(g, "dp", scatter_dimension=d, axis_index_groups=blocks, tiled=True), d) for g, d in grads
        ]
    return (emb, dx, *[g for g, d in grads])


def solution(mesh):
    rem = mesh.shape["dp"] // SHARDS
    plan = plan_of()

    def whole(*args):
        return unpack(rem, *per_device(rem, plan, *args))

    placed = (P(("dp", "section"), None, None), P(("dp", "section")), P(("dp", "section"))) + (P(),) * 13 + (P(("dp", "section"), None),)
    return jax.shard_map(
        whole,
        mesh=mesh,
        in_specs=placed,
        out_specs=(
            P(("dp", "section"), None), P(("dp", "section"), None, None), P(None, "dp"), P(None, "dp"), P(None, "dp", None), P(None, "dp", None),
            P(None, "dp"), P(None, "dp"), P(None, "dp", None), P(None, "dp"), P(None, "dp", None), P(None, "dp"), P("dp"), P("dp", None), P("dp"),
        ),
        check_vma=False,
    )
```

```python
import functools

import jax
import jax.numpy as jnp
from jax import lax
from jax.experimental import pallas as pl
from jax.experimental.pallas import tpu as pltpu
from jax.sharding import PartitionSpec as P

HEADS = 8
EPS = 1e-05
MASKED = -1e30
F32 = jnp.float32
BF16 = jnp.bfloat16
MESH = pl.DeviceIdType.MESH
SHARDS = 8
PIECE = 16
GROUPS_OUT = 7
SLOTS = 3


def mm(left, right):
    return jnp.dot(left, right, preferred_element_type=F32)


def mm_right(left, right):
    return lax.dot_general(left, right, (((1,), (1,)), ((), ())), preferred_element_type=F32)


def flipped(value, mask):
    return value + mask - 2 * mask * ((value // mask) % 2)


def normalised(values):
    centre = values - jnp.mean(values, axis=-1, keepdims=True)
    scale = lax.rsqrt(jnp.mean(centre * centre, axis=-1, keepdims=True) + EPS)
    return centre * scale, scale


def gelu_both(v):
    size = jnp.abs(v)
    t = 1.0 / (1.0 + (0.3275911 * 0.7071067811865476) * size)
    bell = jnp.exp(-0.5 * (v * v))
    poly = t * (
        0.127414796
        + t * (-0.142248368 + t * (0.7107068705 + t * (-0.7265760135 + t * 0.5307027145)))
    )
    tail = poly * bell
    cdf = jnp.where(v >= 0, 1.0 - tail, tail)
    return v * cdf, cdf + v * (bell * 0.3989422804014327)


PARTS = {
    "a": (slice(0, 2), ("x", "y", "zl", "zh")),
    "b": (slice(2, 3), ("y", "zl", "x", "zh")),
    "c": (slice(3, 4), ("zl", "zh", "x", "y")),
}
AXES = ("y", "zh", "zl", "x")


def kernel(rem, plan, *refs):
    (
        pieces_ref, counts_ref, groups_ref, table_ref, again_ref, abias_ref, fgain_ref, ubias_ref, dbias_ref,
        egain_ref, pbias_ref, cot_ref, wqkv_hbm, wout_hbm, wup_hbm, wdown_hbm, wpool_hbm,
        emb_ref, dx_ref, fin_ref, small_ref,
        wqkv, wout, wup, wdown, wpool, es, ex, x0, hs, nb, qkv, prob, ctx, act, dg, dyb, dqkv, d_scores, pairs, wide, tmp, npool, upool,
        g_buf, r0, ra, rb, rc, f_buf, s_buf, w_sem, send_sem, recv_sem, out_sem,
    ) = refs
    slots, entries, width = pieces_ref.shape
    layers = again_ref.shape[0]
    token_rows = slots * entries
    b = lax.axis_index("dp") // rem
    s = lax.axis_index("section")
    bits = {"zh": b // 4, "zl": (b // 2) % 2, "x": b % 2, "y": s // 2, "core": s % 2}
    dp_mask = {"zh": 4 * rem, "zl": 2 * rem, "x": rem, "y": 0, "core": 0}
    sec_mask = {"zh": 0, "zl": 0, "x": 0, "y": 2, "core": 1}

    def partner(axis):
        d, e = lax.axis_index("dp"), lax.axis_index("section")
        return (
            flipped(d, dp_mask[axis]) if dp_mask[axis] else d,
            flipped(e, sec_mask[axis]) if sec_mask[axis] else e,
        )

    barrier = pltpu.get_barrier_semaphore()
    for axis in bits:
        pl.semaphore_signal(barrier, inc=1, device_id=partner(axis), device_id_type=MESH)

    loads = {}
    order = []
    for layer in range(layers):
        order += [("qkv", layer, wqkv_hbm, wqkv), ("out", layer, wout_hbm, wout), ("up", layer, wup_hbm, wup), ("down", layer, wdown_hbm, wdown)]
    for at, (name, layer, source, target) in enumerate(order):
        loads[name, layer] = pltpu.make_async_copy(source.at[layer], target.at[layer], w_sem.at[at])
        loads[name, layer].start()
    loads["pool", 0] = pltpu.make_async_copy(wpool_hbm, wpool, w_sem.at[len(order)])
    loads["pool", 0].start()

    def ready(name, layer):
        loads.pop((name, layer)).wait()

    def rows(j):
        return pl.ds(pl.multiple_of(j * entries, entries), entries)

    def column(row_ref):
        eye = lax.broadcasted_iota(jnp.int32, (entries, entries), 0) == lax.broadcasted_iota(
            jnp.int32, (entries, entries), 1
        )
        row = row_ref[...].astype(F32)
        return jnp.sum(jnp.where(eye, row, 0.0), axis=1, keepdims=True)

    count = column(counts_ref)
    group = column(groups_ref)

    head_of = lax.broadcasted_iota(jnp.int32, (width, 128), 0) // (width // HEADS)
    lane_of = lax.broadcasted_iota(jnp.int32, (width, 128), 1) % 64
    head_of_t = lax.broadcasted_iota(jnp.int32, (128, width), 1) // (width // HEADS)
    lane_of_t = lax.broadcasted_iota(jnp.int32, (128, width), 0)
    scaling = (width // HEADS) ** -0.5
    lane_slot = (lax.broadcasted_iota(jnp.int32, (token_rows, 128), 1) % 64) // HEADS
    es[...] = jnp.where(lane_of % HEADS == head_of, scaling, 0.0).astype(BF16)
    for j in range(slots):
        ex[j] = jnp.where(lane_of_t - head_of_t == j * HEADS, 1.0, 0.0).astype(BF16)
    live_lanes = (
        (lax.broadcasted_iota(jnp.int32, (entries, 128), 1) % 64) // HEADS
    ).astype(F32) < count

    group_rows = jnp.zeros((entries, width), F32)
    for g in range(table_ref.shape[0]):
        group_rows = jnp.where(group == g, table_ref[g : g + 1, :].astype(F32), group_rows)
    for j in range(slots):
        x0[j * entries : (j + 1) * entries, :] = pieces_ref[j].astype(F32) + group_rows

    def norm_rows(source, gain):
        for j in range(slots):
            n, _r = normalised(source[rows(j), :].astype(F32))
            nb[rows(j), :] = (n * gain).astype(BF16)

    def rolled(value, op):
        for shift in (8, 16, 32):
            value = op(value, pltpu.roll(value, shift, 1))
        return value

    def spread_rows(block, value):
        n = value.shape[-1]
        return (value.reshape(slots, entries, n) * block[None]).reshape(token_rows, n)

    def pair_sums(key_rows, query_rows):
        for j in range(slots):
            pairs[j * token_rows : (j + 1) * token_rows, :] = spread_rows(key_rows[rows(j), :], query_rows)
        sums = mm(pairs[...], es[...])
        total = jnp.zeros((token_rows, 128), F32)
        for j in range(slots):
            total = jnp.where(lane_slot == j, sums[j * token_rows : (j + 1) * token_rows, :], total)
        return total

    def attention_forward(layer, source, target):
        norm_rows(source, again_ref[layer : layer + 1, :].astype(F32))
        ready("qkv", layer)
        for t in range(3):
            cols = pl.ds(t * width, width)
            qkv[layer, :, cols] = mm(nb[...], wqkv[layer, :, cols]).astype(BF16)
        scores = pair_sums(qkv.at[layer, :, pl.ds(width, width)], qkv[layer, :, 0:width])
        scores = jnp.where(live_lanes[None], scores.reshape(slots, entries, 128), MASKED).reshape(token_rows, 128)
        raised = jnp.exp(scores - rolled(scores, jnp.maximum))
        p = raised / rolled(raised, jnp.add)
        prob[layer] = p
        p_low = p.astype(BF16)

        @pl.loop(0, width // 128)
        def _(c):
            lanes = pl.ds(pl.multiple_of(c * 128, 128), 128)
            v_lanes = pl.ds(pl.multiple_of(2 * width + c * 128, 128), 128)
            total = jnp.zeros((token_rows, 128), F32)
            for j in range(slots):
                total += spread_rows(qkv[layer, rows(j), v_lanes].astype(F32), mm(p_low, ex[j, :, lanes]))
            ctx[layer, :, lanes] = total.astype(BF16)

        ready("out", layer)
        bias = abias_ref[layer : layer + 1, :].astype(F32)
        hs[target] = (source[...].astype(F32) + mm(ctx[layer], wout[layer]) + bias).astype(BF16)

    def ffn_forward(layer, source, target):
        norm_rows(source, fgain_ref[layer : layer + 1, :].astype(F32))
        ready("up", layer)

        for t in range(wup.shape[2] // 256):
            cols = pl.ds(t * 256, 256)
            inner = mm(nb[...], wup[layer, :, cols]) + ubias_ref[layer : layer + 1, cols].astype(F32)
            activated, slope = gelu_both(inner)
            act[layer, :, cols] = activated.astype(BF16)
            dg[layer, :, cols] = slope.astype(BF16)

        ready("down", layer)
        bias = dbias_ref[layer : layer + 1, :].astype(F32)
        hs[target] = (source[...].astype(F32) + mm(act[layer], wdown[layer]) + bias).astype(BF16)

    def put_columns(slot, quantum, value):
        block = value.astype(BF16)
        for o in range(SHARDS):
            for y in range(2):
                for c in range(2):
                    at = o * 64 + y * 32 + c * PIECE
                    g_buf[slot, quantum, c, y, o // 4, (o // 2) % 2, o % 2] = block[at : at + PIECE]

    def put_down(slot, t, value):
        block = value.astype(BF16)
        for half in range(2):
            for k in range(4):
                for y in range(2):
                    for c in range(2):
                        at = half * 256 + k * 64 + y * 32 + c * PIECE
                        g_buf[slot, k, c, y, t // 2, t % 2, half] = block[at : at + PIECE]

    def col_sum(value):
        return jnp.sum(value, axis=0, keepdims=True)

    part_buffers = {"a": ra, "b": rb, "c": rc}
    copies = sorted({item[1:] for item in plan if item[0] == "start"})

    def views_of(stage, lo, hi, part):
        core, y = bits["core"], bits["y"]
        if stage == 0:
            slot = lo % SLOTS
            return "core", g_buf.at[slot, :, 1 - core], g_buf.at[slot, :, core], r0.at[lo]
        if stage <= 4:
            quanta, dims = PARTS[part]
            axis = dims[stage - 1]
            left = [a for a in AXES if a not in dims[: stage - 1]]
            buffers = part_buffers[part]
            lead = (slice(lo, hi), quanta if stage == 1 else slice(None))
            before = r0 if stage == 1 else buffers[stage - 2]

            def half(index):
                return before.at[lead + tuple(index if a == axis else slice(None) for a in left)]

            return axis, half(1 - bits[axis]), half(bits[axis]), buffers[stage - 1].at[lo:hi]
        if stage == 5:
            view = f_buf.at[lo:hi, :, y, core]
            return "y", view, None, view
        if stage == 6:
            view = f_buf.at[lo:hi, :, :, core]
            return "core", view, None, view
        return ("core", "x", "y", "zl", "zh")[lo], s_buf.at[2 * lo], s_buf.at[2 * lo], s_buf.at[2 * lo + 1]

    def copy_of(key):
        axis, source, mine, landing = views_of(*key)
        at = copies.index(key)
        return pltpu.make_async_remote_copy(
            src_ref=source,
            dst_ref=landing,
            send_sem=send_sem.at[at],
            recv_sem=recv_sem.at[at],
            device_id=partner(axis),
            device_id_type=MESH,
        )

    def start(*key):
        copy_of(key).start()

    def finish(*key):
        stage, lo, hi, part = key
        axis, source, mine, landing = views_of(*key)
        copy_of(key).wait()
        if stage < 4:
            landing[...] = landing[...] + mine[...]
        elif stage == 4:
            f_buf[lo:hi, PARTS[part][0], bits["y"], bits["core"]] = landing[...] + mine[...]
        elif stage == 7:
            s_buf[2 * lo + 2] = landing[...] + mine[...]

    def put_small(at, value):
        s_buf[0, pl.ds(at, value.shape[0]), :] = value

    def forward_attention(layer):
        attention_forward(layer, x0 if layer == 0 else hs.at[2 * layer - 1], 2 * layer)

    def forward_feed(layer):
        ffn_forward(layer, hs.at[2 * layer], 2 * layer + 1)

    def pool_forward():
        live_sum = jnp.zeros((entries, width), F32)
        for j in range(slots):
            n, _r = normalised(hs[2 * layers - 1, rows(j), :].astype(F32))
            live_sum += jnp.where(count > j, n, 0.0)
        npool[...] = live_sum / count
        pooled = (npool[...] * egain_ref[...].astype(F32)).astype(BF16)
        pooled_t = pooled.astype(F32).T.astype(BF16)
        ready("pool", 0)
        for k in range(4):
            put_columns(0, k, mm(pooled_t, cot_ref[:, k * width : (k + 1) * width]))

    def embed():
        pooled = (npool[...] * egain_ref[...].astype(F32)).astype(BF16)
        for k in range(4):
            cols = slice(k * width, (k + 1) * width)
            emb_ref[:, cols] = (mm(pooled, wpool[:, cols]) + pbias_ref[:, cols].astype(F32)).astype(BF16)

    def pool_backward():
        for k in range(4):
            put_small(17 + k, col_sum(cot_ref[:, k * width : (k + 1) * width].astype(F32)))
        d_pooled = mm_right(cot_ref[...], wpool[...]).astype(BF16).astype(F32)
        put_small(16, col_sum(d_pooled * npool[...]))
        upool[...] = d_pooled * egain_ref[...].astype(F32) / count
        for j in range(slots):
            n, r = normalised(hs[2 * layers - 1, rows(j), :].astype(F32))
            u = jnp.where(count > j, upool[...], 0.0)
            d = r * (u - jnp.mean(u, axis=-1, keepdims=True) - n * jnp.mean(u * n, axis=-1, keepdims=True))
            dyb[rows(j), :] = d.astype(BF16)

    def norm_backward(source, gain, at, keep_wide):
        total = jnp.zeros((entries, width), F32)
        for j in range(slots):
            n, r = normalised(source[rows(j), :].astype(F32))
            d_normed = wide[rows(j), :]
            u = d_normed * gain
            d = r * (u - jnp.mean(u, axis=-1, keepdims=True) - n * jnp.mean(u * n, axis=-1, keepdims=True))
            d_h = dyb[rows(j), :].astype(F32) + d
            dyb[rows(j), :] = d_h.astype(BF16)
            if keep_wide:
                wide[rows(j), :] = d_h
            total += d_normed * n
        put_small(at, col_sum(total))

    def dy_sum(at):
        put_small(at, col_sum(dyb[...].astype(F32)))

    def turned(value):
        return value.astype(F32).T.astype(BF16)

    def down_grad(layer, slot, part):
        if part == 0:
            dy_sum(8 * layer + 3)
        for t in (2 * part, 2 * part + 1):
            cols = pl.ds(t * width, width)
            put_down(slot, t, mm(turned(act[layer, :, cols]), dyb[...]))

    def up_grad(layer, slot, source, t):
        gain = fgain_ref[layer : layer + 1, :].astype(F32)
        if t == 0:
            norm_rows(source, gain)
            tmp[...] = turned(nb[...])
        if t < 4:
            cols = pl.ds(t * width, width)
            d_act = mm_right(dyb[...], wdown[layer, cols, :])
            d_inner = (d_act * dg[layer, :, cols].astype(F32)).astype(BF16)
            put_small(8 * layer + 4 + t, col_sum(d_inner.astype(F32)))
            put_columns(slot, t, mm(tmp[...], d_inner))
            dqkv[:, cols] = d_inner
        else:
            wide[...] = mm_right(dqkv[...], wup[layer])
            norm_backward(source, gain, 8 * layer + 2, False)

    def out_grad(layer, slot):
        dy_sum(8 * layer + 1)
        put_columns(slot, 3, mm(turned(ctx[layer]), dyb[...]))
        nb[...] = mm_right(dyb[...], wout[layer]).astype(BF16)

    def score_grad(layer):
        d_prob = pair_sums(qkv.at[layer, :, pl.ds(2 * width, width)], nb[...]) * (1.0 / scaling)
        p = prob[layer]
        mixed = p * d_prob
        d_scores[...] = (mixed - p * rolled(mixed, jnp.add)).astype(BF16)

    def head_grad(layer, c):
        def lanes(part):
            return pl.ds(part * width + c * 128, 128)

        p_low = prob[layer].astype(BF16)
        d_q = jnp.zeros((token_rows, 128), F32)
        for j in range(slots):
            weights = mm(p_low, ex[j, :, lanes(0)])
            d_v = jnp.sum((weights * nb[:, lanes(0)].astype(F32)).reshape(slots, entries, 128), axis=0)
            weights = mm(d_scores[...], ex[j, :, lanes(0)])
            d_q += spread_rows(qkv[layer, rows(j), lanes(1)].astype(F32), weights)
            d_k = jnp.sum((weights * qkv[layer, :, lanes(0)].astype(F32)).reshape(slots, entries, 128), axis=0)
            dqkv[rows(j), lanes(1)] = (d_k * scaling).astype(BF16)
            dqkv[rows(j), lanes(2)] = d_v.astype(BF16)
        dqkv[:, lanes(0)] = (d_q * scaling).astype(BF16)

    def qkv_grad(layer, slot, source, t):
        gain = again_ref[layer : layer + 1, :].astype(F32)
        if t == 0:
            norm_rows(source, gain)
            tmp[...] = turned(nb[...])
        if t < 3:
            put_columns(slot, t, mm(tmp[...], dqkv[:, t * width : (t + 1) * width]))
        else:
            wide[...] = mm_right(dqkv[:, 0 : 3 * width], wqkv[layer])
            norm_backward(source, gain, 8 * layer, layer == 0)

    def finish_input():
        sums = jnp.zeros((entries, width), F32)
        for j in range(slots):
            sums += wide[j * entries : (j + 1) * entries, :]
            dx_ref[j] = wide[j * entries : (j + 1) * entries, :].astype(BF16)
        for g in range(table_ref.shape[0]):
            put_small(24 + g, col_sum(jnp.where(group == g, sums, 0.0)))

    s_buf[0] = jnp.zeros(s_buf.shape[1:], F32)

    computations = {
        "af0": lambda: forward_attention(0),
        "ff0": lambda: forward_feed(0),
        "af1": lambda: forward_attention(1),
        "ff1": lambda: forward_feed(1),
        "pool": pool_forward,
        "embed": embed,
        "pool_backward": pool_backward,
        "input": finish_input,
    }
    for layer in range(layers):
        first = 1 if layer == 1 else 4
        feed_source = hs.at[2 * layer]
        attn_source = hs.at[1] if layer == 1 else x0
        down, up, attn = (first % SLOTS, (first + 1) % SLOTS, (first + 2) % SLOTS)
        for t in range(2):
            computations["down", layer, t] = functools.partial(down_grad, layer, down, t)
        for t in range(5):
            computations["up", layer, t] = functools.partial(up_grad, layer, up, feed_source, t)
        computations["out", layer] = functools.partial(out_grad, layer, attn)
        computations["score", layer] = functools.partial(score_grad, layer)
        for t in range(4):
            computations["head", layer, t] = functools.partial(head_grad, layer, t)
            computations["qkv", layer, t] = functools.partial(qkv_grad, layer, attn, attn_source, t)
    entered = all(p[0] == "compute" for p in plan)
    if entered:
        pl.semaphore_wait(barrier, 5)
    for item in plan:
        if item[0] == "compute":
            computations[item[1]]()
            continue
        if not entered:
            pl.semaphore_wait(barrier, 5)
            entered = True
        if item[0] == "start":
            start(*item[1:])
        elif item[0] == "finish":
            finish(*item[1:])
    for copy in loads.values():
        copy.wait()
    done = pltpu.make_async_copy(f_buf, fin_ref, out_sem)
    done.start()
    small_ref[...] = s_buf[10]
    done.wait()


def plan_of():
    return (
        ("compute", "af0"),
        ("compute", "ff0"),
        ("compute", "af1"),
        ("compute", "ff1"),
        ("compute", "pool"),
        ("start", 0, 0, 1, ""),
        ("compute", "pool_backward"),
        ("compute", ("down", 1, 0)),
        ("compute", ("down", 1, 1)),
        ("start", 0, 1, 2, ""),
        ("finish", 0, 0, 1, ""),
        ("start", 1, 0, 1, "a"),
        ("start", 1, 0, 1, "b"),
        ("start", 1, 0, 1, "c"),
        ("compute", ("up", 1, 0)),
        ("compute", ("up", 1, 1)),
        ("compute", ("up", 1, 2)),
        ("finish", 0, 1, 2, ""),
        ("start", 1, 1, 2, "c"),
        ("start", 1, 1, 2, "a"),
        ("start", 1, 1, 2, "b"),
        ("compute", ("up", 1, 3)),
        ("start", 0, 2, 3, ""),
        ("compute", ("up", 1, 4)),
        ("finish", 1, 0, 1, "b"),
        ("start", 2, 0, 1, "b"),
        ("finish", 1, 0, 1, "c"),
        ("start", 2, 0, 1, "c"),
        ("compute", ("out", 1)),
        ("compute", ("score", 1)),
        ("finish", 0, 2, 3, ""),
        ("start", 1, 2, 3, "b"),
        ("start", 1, 2, 3, "c"),
        ("compute", ("head", 1, 0)),
        ("finish", 1, 1, 2, "c"),
        ("start", 2, 1, 2, "c"),
        ("finish", 1, 1, 2, "b"),
        ("start", 2, 1, 2, "b"),
        ("compute", ("head", 1, 1)),
        ("compute", ("head", 1, 2)),
        ("finish", 1, 0, 1, "a"),
        ("start", 2, 0, 1, "a"),
        ("start", 1, 2, 3, "a"),
        ("finish", 2, 0, 1, "b"),
        ("compute", ("head", 1, 3)),
        ("finish", 2, 0, 1, "c"),
        ("compute", ("qkv", 1, 0)),
        ("compute", ("qkv", 1, 1)),
        ("compute", ("qkv", 1, 2)),
        ("start", 0, 3, 4, ""),
        ("finish", 1, 1, 2, "a"),
        ("start", 2, 1, 2, "a"),
        ("finish", 1, 2, 3, "b"),
        ("start", 2, 2, 3, "b"),
        ("compute", ("qkv", 1, 3)),
        ("compute", ("down", 0, 0)),
        ("finish", 2, 1, 2, "b"),
        ("finish", 0, 3, 4, ""),
        ("start", 1, 3, 4, "b"),
        ("start", 1, 3, 4, "a"),
        ("start", 1, 3, 4, "c"),
        ("finish", 2, 0, 1, "a"),
        ("finish", 2, 1, 2, "c"),
        ("compute", ("down", 0, 1)),
        ("start", 0, 4, 5, ""),
        ("finish", 1, 2, 3, "c"),
        ("start", 2, 2, 3, "c"),
        ("compute", ("up", 0, 0)),
        ("finish", 2, 2, 3, "b"),
        ("compute", ("up", 0, 1)),
        ("finish", 1, 2, 3, "a"),
        ("start", 3, 0, 3, "b"),
        ("start", 2, 2, 3, "a"),
        ("finish", 0, 4, 5, ""),
        ("start", 1, 4, 5, "c"),
        ("start", 1, 4, 5, "b"),
        ("start", 1, 4, 5, "a"),
        ("finish", 2, 1, 2, "a"),
        ("compute", ("up", 0, 2)),
        ("compute", ("up", 0, 3)),
        ("start", 0, 5, 6, ""),
        ("finish", 1, 3, 4, "b"),
        ("start", 2, 3, 4, "b"),
        ("compute", ("up", 0, 4)),
        ("finish", 2, 2, 3, "c"),
        ("finish", 1, 3, 4, "c"),
        ("start", 2, 3, 4, "c"),
        ("compute", ("out", 0)),
        ("finish", 0, 5, 6, ""),
        ("start", 1, 5, 6, "b"),
        ("start", 1, 5, 6, "c"),
        ("compute", ("score", 0)),
        ("compute", ("head", 0, 0)),
        ("finish", 1, 4, 5, "c"),
        ("start", 2, 4, 5, "c"),
        ("compute", ("head", 0, 1)),
        ("finish", 2, 2, 3, "a"),
        ("start", 3, 0, 3, "a"),
        ("finish", 3, 0, 3, "b"),
        ("start", 4, 0, 3, "b"),
        ("finish", 1, 4, 5, "b"),
        ("finish", 2, 3, 4, "b"),
        ("compute", ("head", 0, 2)),
        ("finish", 1, 3, 4, "a"),
        ("start", 3, 0, 3, "c"),
        ("start", 2, 3, 4, "a"),
        ("start", 1, 5, 6, "a"),
        ("compute", ("head", 0, 3)),
        ("finish", 2, 3, 4, "c"),
        ("compute", ("qkv", 0, 0)),
        ("finish", 1, 5, 6, "b"),
        ("compute", ("qkv", 0, 1)),
        ("compute", ("qkv", 0, 2)),
        ("start", 0, 6, 7, ""),
        ("compute", ("qkv", 0, 3)),
        ("finish", 1, 4, 5, "a"),
        ("start", 2, 4, 5, "a"),
        ("compute", "input"),
        ("start", 7, 0, 1, ""),
        ("compute", "embed"),
        ("finish", 0, 6, 7, ""),
        ("start", 1, 6, 7, "a"),
        ("start", 1, 6, 7, "b"),
        ("finish", 2, 3, 4, "a"),
        ("finish", 1, 5, 6, "c"),
        ("start", 2, 4, 5, "b"),
        ("start", 1, 6, 7, "c"),
        ("start", 2, 5, 6, "c"),
        ("finish", 2, 4, 5, "c"),
        ("finish", 7, 0, 1, ""),
        ("finish", 4, 0, 3, "b"),
        ("finish", 3, 0, 3, "c"),
        ("start", 4, 0, 3, "c"),
        ("finish", 3, 0, 3, "a"),
        ("start", 4, 0, 3, "a"),
        ("start", 2, 5, 6, "b"),
        ("finish", 2, 4, 5, "a"),
        ("start", 3, 3, 5, "a"),
        ("finish", 4, 0, 3, "c"),
        ("finish", 2, 4, 5, "b"),
        ("finish", 1, 6, 7, "b"),
        ("finish", 1, 5, 6, "a"),
        ("start", 7, 1, 2, ""),
        ("start", 3, 3, 5, "c"),
        ("start", 3, 3, 5, "b"),
        ("start", 2, 5, 6, "a"),
        ("finish", 2, 5, 6, "c"),
        ("start", 3, 5, 6, "c"),
        ("finish", 1, 6, 7, "a"),
        ("start", 2, 6, 7, "a"),
        ("finish", 2, 5, 6, "b"),
        ("start", 2, 6, 7, "b"),
        ("start", 3, 5, 6, "b"),
        ("finish", 1, 6, 7, "c"),
        ("start", 2, 6, 7, "c"),
        ("finish", 3, 5, 6, "c"),
        ("start", 4, 5, 6, "c"),
        ("finish", 2, 5, 6, "a"),
        ("start", 3, 5, 6, "a"),
        ("finish", 4, 0, 3, "a"),
        ("start", 5, 0, 3, ""),
        ("finish", 3, 3, 5, "a"),
        ("start", 4, 3, 5, "a"),
        ("finish", 7, 1, 2, ""),
        ("start", 7, 2, 3, ""),
        ("finish", 3, 3, 5, "c"),
        ("start", 4, 3, 5, "c"),
        ("finish", 3, 3, 5, "b"),
        ("start", 4, 3, 5, "b"),
        ("finish", 3, 5, 6, "b"),
        ("finish", 2, 6, 7, "a"),
        ("start", 3, 6, 7, "a"),
        ("finish", 4, 5, 6, "c"),
        ("finish", 2, 6, 7, "b"),
        ("start", 3, 6, 7, "b"),
        ("finish", 2, 6, 7, "c"),
        ("start", 4, 5, 6, "b"),
        ("start", 3, 6, 7, "c"),
        ("finish", 4, 3, 5, "c"),
        ("finish", 3, 6, 7, "b"),
        ("start", 4, 6, 7, "b"),
        ("finish", 7, 2, 3, ""),
        ("start", 7, 3, 4, ""),
        ("finish", 3, 5, 6, "a"),
        ("start", 4, 5, 6, "a"),
        ("finish", 4, 3, 5, "b"),
        ("finish", 4, 3, 5, "a"),
        ("start", 5, 3, 5, ""),
        ("finish", 3, 6, 7, "a"),
        ("start", 4, 6, 7, "a"),
        ("finish", 5, 0, 3, ""),
        ("start", 6, 0, 3, ""),
        ("finish", 3, 6, 7, "c"),
        ("start", 4, 6, 7, "c"),
        ("finish", 4, 5, 6, "b"),
        ("finish", 4, 6, 7, "b"),
        ("finish", 6, 0, 3, ""),
        ("finish", 4, 5, 6, "a"),
        ("start", 5, 5, 6, ""),
        ("finish", 7, 3, 4, ""),
        ("start", 7, 4, 5, ""),
        ("finish", 4, 6, 7, "c"),
        ("finish", 4, 6, 7, "a"),
        ("start", 5, 6, 7, ""),
        ("finish", 5, 3, 5, ""),
        ("start", 6, 3, 5, ""),
        ("finish", 6, 3, 5, ""),
        ("finish", 5, 5, 6, ""),
        ("start", 6, 5, 6, ""),
        ("finish", 6, 5, 6, ""),
        ("finish", 5, 6, 7, ""),
        ("start", 6, 6, 7, ""),
        ("finish", 7, 4, 5, ""),
        ("finish", 6, 6, 7, ""),
    )


def per_device(rem, plan, pieces, counts, groups, table, again, wqkv, wout, abias, fgain, wup, ubias, wdown, dbias, egain, wpool, pbias, cot):
    pieces = jnp.transpose(pieces, (1, 0, 2))
    slots, entries, width = pieces.shape
    hidden = wup.shape[2]
    layers = wqkv.shape[0]
    token_rows = entries * slots
    vmem = pl.BlockSpec(memory_space=pltpu.VMEM)
    hbm = pl.BlockSpec(memory_space=pl.ANY)
    tile = (PIECE, width)

    def buffers(part):
        quanta, dims = PARTS[part]
        size = quanta.stop - quanta.start
        return [pltpu.VMEM((GROUPS_OUT, size) + (2,) * (3 - k) + tile, BF16) for k in range(4)]

    def body(*refs):
        refs = list(refs)
        fixed = 17 + 4 + 25
        head, rest = refs[: fixed], refs[fixed:]
        parts = [rest[4 * k : 4 * k + 4] for k in range(3)]
        kernel(rem, plan, *head, *parts, *rest[12:])

    copies = len({item[1:] for item in plan if item[0] == "start"})
    scratch = [
        pltpu.VMEM(wqkv.shape, BF16), pltpu.VMEM(wout.shape, BF16), pltpu.VMEM(wup.shape, BF16), pltpu.VMEM(wdown.shape, BF16),
        pltpu.VMEM(wpool.shape, BF16), pltpu.VMEM((width, 128), BF16), pltpu.VMEM((slots, 128, width), BF16),
        pltpu.VMEM((token_rows, width), F32), pltpu.VMEM((2 * layers, token_rows, width), BF16),
        pltpu.VMEM((token_rows, width), BF16), pltpu.VMEM((layers, token_rows, 3 * width), BF16), pltpu.VMEM((layers, token_rows, 128), F32),
        pltpu.VMEM((layers, token_rows, width), BF16), pltpu.VMEM((layers, token_rows, hidden), BF16), pltpu.VMEM((layers, token_rows, hidden), BF16),
        pltpu.VMEM((token_rows, width), BF16), pltpu.VMEM((token_rows, hidden), BF16), pltpu.VMEM((token_rows, 128), BF16), pltpu.VMEM((slots * token_rows, width), BF16), pltpu.VMEM((token_rows, width), F32),
        pltpu.VMEM((width, token_rows), BF16), pltpu.VMEM((entries, width), F32), pltpu.VMEM((entries, width), F32),
        pltpu.VMEM((SLOTS, 4, 2, 2, 2, 2, 2) + tile, BF16), pltpu.VMEM((GROUPS_OUT, 4, 2, 2, 2, 2) + tile, BF16),
        *buffers("a"), *buffers("b"), *buffers("c"),
        pltpu.VMEM((GROUPS_OUT, 4, 2, 2) + tile, BF16), pltpu.VMEM((11, 32, width), F32),
        pltpu.SemaphoreType.DMA((4 * layers + 1,)), pltpu.SemaphoreType.DMA((copies,)), pltpu.SemaphoreType.DMA((copies,)), pltpu.SemaphoreType.DMA,
    ]
    emb, dx, fin, small = pl.pallas_call(
        body,
        out_shape=(
            jax.ShapeDtypeStruct((entries, wpool.shape[1]), BF16),
            jax.ShapeDtypeStruct(pieces.shape, BF16),
            jax.ShapeDtypeStruct((GROUPS_OUT, 4, 2, 2) + tile, BF16),
            jax.ShapeDtypeStruct((32, width), F32),
        ),
        in_specs=[vmem] * 12 + [hbm] * 5,
        out_specs=(vmem, vmem, hbm, vmem),
        scratch_shapes=scratch,
        compiler_params=pltpu.CompilerParams(collective_id=0, has_side_effects=True, vmem_limit_bytes=64 * 2**20),
    )(
        pieces, counts.reshape(1, -1), groups.reshape(1, -1), table, again, abias, fgain, ubias, dbias,
        egain.reshape(1, -1), pbias.reshape(1, -1), cot, wqkv, wout, wup, wdown, wpool,
    )
    return emb, dx, fin, small


def unpack_kernel(rem, fin, small, emb, dx, emb_o, dx_o, table_o, again_o, qkv_o, out_o, abias_o, fgain_o, up_o, ubias_o, down_o, dbias_o, egain_o, pool_o, pbias_o):
    part = lax.axis_index("dp") // rem
    width = fin.shape[-1]
    short = width // SHARDS
    emb_o[...] = emb[...]
    dx_o[...] = dx[...]

    def block(group, k):
        return fin[group, k].reshape(4 * PIECE, width).astype(F32)

    def columns(target, group, count):
        for k in range(count):
            target[..., k * width : (k + 1) * width] = block(group, k)

    def share(value):
        return pltpu.roll(value, width - part * short, 1)[:, 0:short]

    columns(pool_o, 0, 4)
    for layer in range(2):
        down, up, attn = (4, 5, 6) if layer == 0 else (1, 2, 3)
        for k in range(4):
            down_o[layer, k * 64 : (k + 1) * 64, :] = block(down, k)
        columns(up_o.at[layer], up, 4)
        columns(qkv_o.at[layer], attn, 3)
        out_o[layer] = block(attn, 3)
        for row, target in enumerate((again_o, abias_o, fgain_o, dbias_o)):
            target[layer : layer + 1, :] = share(small[8 * layer + row : 8 * layer + row + 1, :])
    half = width // 2

    def long_share(first):
        value = small[pl.ds(first + part // 2, 1), :]
        return jnp.where(part % 2 == 0, value[:, 0:half], value[:, half:width])

    for layer in range(2):
        ubias_o[layer : layer + 1, :] = long_share(8 * layer + 4)
    table_o[...] = share(small[24:32, :])
    egain_o[...] = share(small[16:17, :])
    pbias_o[...] = long_share(17)


def unpack(rem, emb, dx, fin, small):
    width = fin.shape[-1]
    short = width // SHARDS

    def f32(*shape):
        return jax.ShapeDtypeStruct(shape, F32)

    emb, dx, *grads = pl.pallas_call(
        functools.partial(unpack_kernel, rem),
        out_shape=(
            jax.ShapeDtypeStruct(emb.shape, BF16), jax.ShapeDtypeStruct(dx.shape, BF16), f32(8, short), f32(2, short), f32(2, 64, 3 * width),
            f32(2, 64, width), f32(2, short), f32(2, short), f32(2, 64, 4 * width), f32(2, 4 * short), f32(2, 256, width), f32(2, short),
            f32(1, short), f32(64, 4 * width), f32(1, 4 * short),
        ),
        compiler_params=pltpu.CompilerParams(vmem_limit_bytes=48 * 2**20),
    )(fin, small, emb, dx)
    grads[10] = grads[10].reshape(-1)
    grads[12] = grads[12].reshape(-1)
    if rem > 1:
        blocks = [list(range(k * rem, (k + 1) * rem)) for k in range(SHARDS)]
        dims = (1,) * 10 + (0,) * 3
        grads = [
            lax.psum_scatter(g, "dp", scatter_dimension=d, axis_index_groups=blocks, tiled=True)
            for g, d in zip(grads, dims)
        ]
    return (emb, jnp.transpose(dx, (1, 0, 2)), *grads)


def solution(mesh):
    rem = mesh.shape["dp"] // SHARDS
    plan = plan_of()

    def whole(*args):
        return unpack(rem, *per_device(rem, plan, *args))

    placed = (P(("dp", "section"), None, None), P(("dp", "section")), P(("dp", "section"))) + (P(),) * 13 + (P(("dp", "section"), None),)
    return jax.shard_map(
        whole,
        mesh=mesh,
        in_specs=placed,
        out_specs=(
            P(("dp", "section"), None), P(("dp", "section"), None, None), P(None, "dp"), P(None, "dp"), P(None, "dp", None), P(None, "dp", None),
            P(None, "dp"), P(None, "dp"), P(None, "dp", None), P(None, "dp"), P(None, "dp", None), P(None, "dp"), P("dp"), P("dp", None), P("dp"),
        ),
        check_vma=False,
    )
```

```python
import functools

import jax
import jax.numpy as jnp
from jax import lax
from jax.experimental import pallas as pl
from jax.experimental.pallas import tpu as pltpu
from jax.sharding import PartitionSpec as P

HEADS = 8
EPS = 1e-05
MASKED = -1e30
F32 = jnp.float32
BF16 = jnp.bfloat16
MESH = pl.DeviceIdType.MESH
SHARDS = 8
PIECE = 16
GROUPS_OUT = 7
SLOTS = 3


def mm(left, right):
    return jnp.dot(left, right, preferred_element_type=F32)


def mm_right(left, right):
    return lax.dot_general(left, right, (((1,), (1,)), ((), ())), preferred_element_type=F32)


def flipped(value, mask):
    return value + mask - 2 * mask * ((value // mask) % 2)


def normalised(values):
    centre = values - jnp.mean(values, axis=-1, keepdims=True)
    scale = lax.rsqrt(jnp.mean(centre * centre, axis=-1, keepdims=True) + EPS)
    return centre * scale, scale


def gelu_both(v):
    size = jnp.abs(v)
    base = 1.0 + (0.3275911 * 0.7071067811865476) * size
    t = 1.0 / base
    bell = jnp.exp(-0.5 * (v * v))
    poly = t * (
        0.127414796
        + t * (-0.142248368 + t * (0.7107068705 + t * (-0.7265760135 + t * 0.5307027145)))
    )
    tail = poly * bell
    cdf = jnp.where(v >= 0, 1.0 - tail, tail)
    return v * cdf, cdf + v * (bell * 0.3989422804014327)


PARTS = {
    "a": (slice(0, 2), ("x", "y", "zl", "zh")),
    "b": (slice(2, 3), ("y", "zl", "x", "zh")),
    "c": (slice(3, 4), ("zl", "zh", "x", "y")),
}
OTHER = {("c", 6): ("y", "zl", "x", "zh")}
AXES = ("y", "zh", "zl", "x")


def kernel(rem, plan, *refs):
    (
        pieces_ref, counts_ref, groups_ref, table_ref, again_ref, abias_ref, fgain_ref, ubias_ref, dbias_ref,
        egain_ref, pbias_ref, cot_ref, wqkv_hbm, wout_hbm, wup_hbm, wdown_hbm, wpool_hbm,
        emb_ref, dx_ref, fin_ref, small_ref,
        wqkv, wout, wup, wdown, wpool, es, ex, x0, hs, nb, qkv, prob, ctx, act, dg, dyb, dqkv, d_scores, pairs, wide, tmp, npool, upool,
        g_buf, r0, ra, rb, rc, f_buf, s_buf, w_sem, send_sem, recv_sem, out_sem,
    ) = refs
    slots, entries, width = pieces_ref.shape
    layers = again_ref.shape[0]
    token_rows = slots * entries
    b = lax.axis_index("dp") // rem
    s = lax.axis_index("section")
    bits = {"zh": b // 4, "zl": (b // 2) % 2, "x": b % 2, "y": s // 2, "core": s % 2}
    dp_mask = {"zh": 4 * rem, "zl": 2 * rem, "x": rem, "y": 0, "core": 0}
    sec_mask = {"zh": 0, "zl": 0, "x": 0, "y": 2, "core": 1}

    def partner(axis):
        d, e = lax.axis_index("dp"), lax.axis_index("section")
        return (
            flipped(d, dp_mask[axis]) if dp_mask[axis] else d,
            flipped(e, sec_mask[axis]) if sec_mask[axis] else e,
        )

    barrier = pltpu.get_barrier_semaphore()
    for axis in bits:
        pl.semaphore_signal(barrier, inc=1, device_id=partner(axis), device_id_type=MESH)

    loads = {}
    order = []
    for layer in range(layers):
        order += [("qkv", layer, wqkv_hbm, wqkv), ("out", layer, wout_hbm, wout), ("up", layer, wup_hbm, wup), ("down", layer, wdown_hbm, wdown)]
    for at, (name, layer, source, target) in enumerate(order):
        loads[name, layer] = pltpu.make_async_copy(source.at[layer], target.at[layer], w_sem.at[at])
        loads[name, layer].start()
    loads["pool", 0] = pltpu.make_async_copy(wpool_hbm, wpool, w_sem.at[len(order)])
    loads["pool", 0].start()

    def ready(name, layer):
        loads.pop((name, layer)).wait()

    def rows(j):
        return pl.ds(pl.multiple_of(j * entries, entries), entries)

    def column(row_ref):
        eye = lax.broadcasted_iota(jnp.int32, (entries, entries), 0) == lax.broadcasted_iota(
            jnp.int32, (entries, entries), 1
        )
        row = row_ref[...].astype(F32)
        return jnp.sum(jnp.where(eye, row, 0.0), axis=1, keepdims=True)

    count = column(counts_ref)
    group = column(groups_ref)

    head_of = lax.broadcasted_iota(jnp.int32, (width, 128), 0) // (width // HEADS)
    lane_of = lax.broadcasted_iota(jnp.int32, (width, 128), 1) % 64
    head_of_t = lax.broadcasted_iota(jnp.int32, (128, width), 1) // (width // HEADS)
    lane_of_t = lax.broadcasted_iota(jnp.int32, (128, width), 0)
    scaling = (width // HEADS) ** -0.5
    lane_slot = (lax.broadcasted_iota(jnp.int32, (token_rows, 128), 1) % 64) // HEADS
    es[...] = jnp.where(lane_of % HEADS == head_of, scaling, 0.0).astype(BF16)
    for j in range(slots):
        ex[j] = jnp.where(lane_of_t - head_of_t == j * HEADS, 1.0, 0.0).astype(BF16)
    live_lanes = (
        (lax.broadcasted_iota(jnp.int32, (entries, 128), 1) % 64) // HEADS
    ).astype(F32) < count

    group_rows = jnp.zeros((entries, width), F32)
    for g in range(table_ref.shape[0]):
        group_rows = jnp.where(group == g, table_ref[g : g + 1, :].astype(F32), group_rows)
    for j in range(slots):
        x0[j * entries : (j + 1) * entries, :] = pieces_ref[j].astype(F32) + group_rows

    def norm_rows(source, gain):
        for j in range(slots):
            n, _r = normalised(source[rows(j), :].astype(F32))
            nb[rows(j), :] = (n * gain).astype(BF16)

    def rolled(value, op):
        for shift in (8, 16, 32):
            value = op(value, pltpu.roll(value, shift, 1))
        return value

    def spread_rows(block, value):
        n = value.shape[-1]
        return (value.reshape(slots, entries, n) * block[None]).reshape(token_rows, n)

    def pair_sums(key_rows, query_rows):
        for j in range(slots):
            pairs[j * token_rows : (j + 1) * token_rows, :] = spread_rows(key_rows[rows(j), :], query_rows)
        sums = mm(pairs[...], es[...])
        total = jnp.zeros((token_rows, 128), F32)
        for j in range(slots):
            total = jnp.where(lane_slot == j, sums[j * token_rows : (j + 1) * token_rows, :], total)
        return total

    def attention_forward(layer, source, target):
        norm_rows(source, again_ref[layer : layer + 1, :].astype(F32))
        ready("qkv", layer)
        for t in range(3):
            cols = pl.ds(t * width, width)
            qkv[layer, :, cols] = mm(nb[...], wqkv[layer, :, cols]).astype(BF16)
        scores = pair_sums(qkv.at[layer, :, pl.ds(width, width)], qkv[layer, :, 0:width])
        scores = jnp.where(live_lanes[None], scores.reshape(slots, entries, 128), MASKED).reshape(token_rows, 128)
        raised = jnp.exp(scores - rolled(scores, jnp.maximum))
        p = raised / rolled(raised, jnp.add)
        prob[layer] = p
        p_low = p.astype(BF16)

        @pl.loop(0, width // 128)
        def _(c):
            lanes = pl.ds(pl.multiple_of(c * 128, 128), 128)
            v_lanes = pl.ds(pl.multiple_of(2 * width + c * 128, 128), 128)
            total = jnp.zeros((token_rows, 128), F32)
            for j in range(slots):
                total += spread_rows(qkv[layer, rows(j), v_lanes].astype(F32), mm(p_low, ex[j, :, lanes]))
            ctx[layer, :, lanes] = total.astype(BF16)

        ready("out", layer)
        bias = abias_ref[layer : layer + 1, :].astype(F32)
        hs[target] = (source[...].astype(F32) + mm(ctx[layer], wout[layer]) + bias).astype(BF16)

    def ffn_forward(layer, source, target):
        norm_rows(source, fgain_ref[layer : layer + 1, :].astype(F32))
        ready("up", layer)
        ready("down", layer)
        wide[...] = source[...].astype(F32) + dbias_ref[layer : layer + 1, :].astype(F32)
        for t in range(wup.shape[2] // 256):
            cols = pl.ds(t * 256, 256)
            inner = mm(nb[...], wup[layer, :, cols]) + ubias_ref[layer : layer + 1, cols].astype(F32)
            activated, slope = gelu_both(inner)
            act[layer, :, cols] = activated.astype(BF16)
            dg[layer, :, cols] = slope.astype(BF16)
            wide[...] += mm(activated.astype(BF16), wdown[layer, cols, :])
        hs[target] = wide[...].astype(BF16)

    def put_columns(slot, quantum, value):
        block = value.astype(BF16)
        for o in range(SHARDS):
            for y in range(2):
                for c in range(2):
                    at = o * 64 + y * 32 + c * PIECE
                    g_buf[slot, quantum, c, y, o // 4, (o // 2) % 2, o % 2] = block[at : at + PIECE]

    def put_down(slot, t, value):
        block = value.astype(BF16)
        for half in range(2):
            for k in range(4):
                for y in range(2):
                    for c in range(2):
                        at = half * 256 + k * 64 + y * 32 + c * PIECE
                        g_buf[slot, k, c, y, t // 2, t % 2, half] = block[at : at + PIECE]

    def col_sum(value):
        return jnp.sum(value, axis=0, keepdims=True)

    part_buffers = {"a": ra, "b": rb, "c": rc}
    copies = sorted({item[1:] for item in plan if item[0] == "start"})

    def views_of(stage, lo, hi, part):
        core, y = bits["core"], bits["y"]
        if stage == 0:
            slot = lo % SLOTS
            return "core", g_buf.at[slot, :, 1 - core], g_buf.at[slot, :, core], r0.at[lo]
        if stage <= 4:
            quanta, dims = PARTS[part][0], OTHER.get((part, lo), PARTS[part][1])
            axis = dims[stage - 1]
            left = [a for a in AXES if a not in dims[: stage - 1]]
            buffers = part_buffers[part]
            lead = (slice(lo, hi), quanta if stage == 1 else slice(None))
            before = r0 if stage == 1 else buffers[stage - 2]

            def half(index):
                return before.at[lead + tuple(index if a == axis else slice(None) for a in left)]

            return axis, half(1 - bits[axis]), half(bits[axis]), buffers[stage - 1].at[lo:hi]
        if stage == 5:
            view = f_buf.at[lo:hi, :, y, core]
            return "y", view, None, view
        if stage == 6:
            view = f_buf.at[lo:hi, :, :, core]
            return "core", view, None, view
        return ("core", "x", "y", "zl", "zh")[lo], s_buf.at[2 * lo], s_buf.at[2 * lo], s_buf.at[2 * lo + 1]

    def copy_of(key):
        axis, source, mine, landing = views_of(*key)
        at = copies.index(key)
        return pltpu.make_async_remote_copy(
            src_ref=source,
            dst_ref=landing,
            send_sem=send_sem.at[at],
            recv_sem=recv_sem.at[at],
            device_id=partner(axis),
            device_id_type=MESH,
        )

    def start(*key):
        copy_of(key).start()

    def finish(*key):
        stage, lo, hi, part = key
        axis, source, mine, landing = views_of(*key)
        copy_of(key).wait()
        if stage < 4:
            landing[...] = landing[...] + mine[...]
        elif stage == 4:
            f_buf[lo:hi, PARTS[part][0], bits["y"], bits["core"]] = landing[...] + mine[...]
        elif stage == 7:
            s_buf[2 * lo + 2] = landing[...] + mine[...]

    def put_small(at, value):
        s_buf[0, pl.ds(at, value.shape[0]), :] = value

    def forward_attention(layer):
        attention_forward(layer, x0 if layer == 0 else hs.at[2 * layer - 1], 2 * layer)

    def forward_feed(layer):
        ffn_forward(layer, hs.at[2 * layer], 2 * layer + 1)

    def pool_forward():
        live_sum = jnp.zeros((entries, width), F32)
        for j in range(slots):
            n, _r = normalised(hs[2 * layers - 1, rows(j), :].astype(F32))
            live_sum += jnp.where(count > j, n, 0.0)
        npool[...] = live_sum / count
        pooled = (npool[...] * egain_ref[...].astype(F32).reshape(1, width)).astype(BF16)
        pooled_t = pooled.astype(F32).T.astype(BF16)
        ready("pool", 0)
        for k in range(4):
            put_columns(0, k, mm(pooled_t, cot_ref[:, k * width : (k + 1) * width]))

    def embed():
        pooled = (npool[...] * egain_ref[...].astype(F32).reshape(1, width)).astype(BF16)
        for k in range(4):
            cols = slice(k * width, (k + 1) * width)
            emb_ref[:, cols] = (mm(pooled, wpool[:, cols]) + pbias_ref[cols].astype(F32).reshape(1, width)).astype(BF16)

    def pool_backward():
        for k in range(4):
            put_small(17 + k, col_sum(cot_ref[:, k * width : (k + 1) * width].astype(F32)))
        d_pooled = mm_right(cot_ref[...], wpool[...]).astype(BF16).astype(F32)
        put_small(16, col_sum(d_pooled * npool[...]))
        upool[...] = d_pooled * egain_ref[...].astype(F32).reshape(1, width) / count
        for j in range(slots):
            n, r = normalised(hs[2 * layers - 1, rows(j), :].astype(F32))
            u = jnp.where(count > j, upool[...], 0.0)
            d = r * (u - jnp.mean(u, axis=-1, keepdims=True) - n * jnp.mean(u * n, axis=-1, keepdims=True))
            dyb[rows(j), :] = d.astype(BF16)

    def norm_backward(source, gain, at, keep_wide):
        total = jnp.zeros((entries, width), F32)
        for j in range(slots):
            n, r = normalised(source[rows(j), :].astype(F32))
            d_normed = wide[rows(j), :]
            u = d_normed * gain
            d = r * (u - jnp.mean(u, axis=-1, keepdims=True) - n * jnp.mean(u * n, axis=-1, keepdims=True))
            d_h = dyb[rows(j), :].astype(F32) + d
            dyb[rows(j), :] = d_h.astype(BF16)
            if keep_wide:
                wide[rows(j), :] = d_h
            total += d_normed * n
        put_small(at, col_sum(total))

    def dy_sum(at):
        put_small(at, col_sum(dyb[...].astype(F32)))

    def turned(value):
        return value.astype(F32).T.astype(BF16)

    def down_grad(layer, slot, part):
        if part == 0:
            dy_sum(8 * layer + 3)
        for t in (2 * part, 2 * part + 1):
            cols = pl.ds(t * width, width)
            put_down(slot, t, mm(turned(act[layer, :, cols]), dyb[...]))

    def up_grad(layer, slot, source, t):
        gain = fgain_ref[layer : layer + 1, :].astype(F32)
        if t == 0:
            norm_rows(source, gain)
            tmp[...] = turned(nb[...])
        if t < 4:
            cols = pl.ds(t * width, width)
            d_act = mm_right(dyb[...], wdown[layer, cols, :])
            d_inner = (d_act * dg[layer, :, cols].astype(F32)).astype(BF16)
            put_small(8 * layer + 4 + t, col_sum(d_inner.astype(F32)))
            put_columns(slot, t, mm(tmp[...], d_inner))
            dqkv[:, cols] = d_inner
        else:
            wide[...] = mm_right(dqkv[...], wup[layer])
            norm_backward(source, gain, 8 * layer + 2, False)

    def out_grad(layer, slot):
        dy_sum(8 * layer + 1)
        put_columns(slot, 3, mm(turned(ctx[layer]), dyb[...]))
        nb[...] = mm_right(dyb[...], wout[layer]).astype(BF16)

    def score_grad(layer):
        d_prob = pair_sums(qkv.at[layer, :, pl.ds(2 * width, width)], nb[...]) * (1.0 / scaling)
        p = prob[layer]
        mixed = p * d_prob
        d_scores[...] = (mixed - p * rolled(mixed, jnp.add)).astype(BF16)

    def head_grad(layer, c):
        def lanes(part):
            return pl.ds(part * width + c * 128, 128)

        p_low = prob[layer].astype(BF16)
        d_q = jnp.zeros((token_rows, 128), F32)
        for j in range(slots):
            weights = mm(p_low, ex[j, :, lanes(0)])
            d_v = jnp.sum((weights * nb[:, lanes(0)].astype(F32)).reshape(slots, entries, 128), axis=0)
            weights = mm(d_scores[...], ex[j, :, lanes(0)])
            d_q += spread_rows(qkv[layer, rows(j), lanes(1)].astype(F32), weights)
            d_k = jnp.sum((weights * qkv[layer, :, lanes(0)].astype(F32)).reshape(slots, entries, 128), axis=0)
            dqkv[rows(j), lanes(1)] = (d_k * scaling).astype(BF16)
            dqkv[rows(j), lanes(2)] = d_v.astype(BF16)
        dqkv[:, lanes(0)] = (d_q * scaling).astype(BF16)

    def qkv_grad(layer, slot, source, t):
        gain = again_ref[layer : layer + 1, :].astype(F32)
        if t == 0:
            norm_rows(source, gain)
            tmp[...] = turned(nb[...])
        if t < 3:
            put_columns(slot, t, mm(tmp[...], dqkv[:, t * width : (t + 1) * width]))
        else:
            wide[...] = mm_right(dqkv[:, 0 : 3 * width], wqkv[layer])
            norm_backward(source, gain, 8 * layer, layer == 0)

    def finish_input():
        sums = jnp.zeros((entries, width), F32)
        for j in range(slots):
            sums += wide[j * entries : (j + 1) * entries, :]
            dx_ref[j] = wide[j * entries : (j + 1) * entries, :].astype(BF16)
        for g in range(table_ref.shape[0]):
            put_small(24 + g, col_sum(jnp.where(group == g, sums, 0.0)))

    s_buf[0] = jnp.zeros(s_buf.shape[1:], F32)

    computations = {
        "af0": lambda: forward_attention(0),
        "ff0": lambda: forward_feed(0),
        "af1": lambda: forward_attention(1),
        "ff1": lambda: forward_feed(1),
        "pool": pool_forward,
        "embed": embed,
        "pool_backward": pool_backward,
        "input": finish_input,
    }
    for layer in range(layers):
        first = 1 if layer == 1 else 4
        feed_source = hs.at[2 * layer]
        attn_source = hs.at[1] if layer == 1 else x0
        down, up, attn = (first % SLOTS, (first + 1) % SLOTS, (first + 2) % SLOTS)
        for t in range(2):
            computations["down", layer, t] = functools.partial(down_grad, layer, down, t)
        for t in range(5):
            computations["up", layer, t] = functools.partial(up_grad, layer, up, feed_source, t)
        computations["out", layer] = functools.partial(out_grad, layer, attn)
        computations["score", layer] = functools.partial(score_grad, layer)
        for t in range(4):
            computations["head", layer, t] = functools.partial(head_grad, layer, t)
            computations["qkv", layer, t] = functools.partial(qkv_grad, layer, attn, attn_source, t)
    entered = all(p[0] == "compute" for p in plan)
    if entered:
        pl.semaphore_wait(barrier, 5)
    for item in plan:
        if item[0] == "compute":
            computations[item[1]]()
            continue
        if not entered:
            pl.semaphore_wait(barrier, 5)
            entered = True
        if item[0] == "start":
            start(*item[1:])
        elif item[0] == "finish":
            finish(*item[1:])
    for copy in loads.values():
        copy.wait()
    done = pltpu.make_async_copy(f_buf, fin_ref, out_sem)
    done.start()
    small_ref[...] = s_buf[10]
    done.wait()


def plan_of():
    return (
        ("compute", "af0"),
        ("compute", "ff0"),
        ("compute", "af1"),
        ("compute", "ff1"),
        ("compute", "pool"),
        ("start", 0, 0, 1, ""),
        ("compute", "pool_backward"),
        ("compute", ("down", 1, 0)),
        ("compute", ("down", 1, 1)),
        ("start", 0, 1, 2, ""),
        ("finish", 0, 0, 1, ""),
        ("start", 1, 0, 1, "a"),
        ("start", 1, 0, 1, "b"),
        ("start", 1, 0, 1, "c"),
        ("compute", ("up", 1, 0)),
        ("compute", ("up", 1, 1)),
        ("compute", ("up", 1, 2)),
        ("finish", 0, 1, 2, ""),
        ("start", 1, 1, 2, "a"),
        ("start", 1, 1, 2, "b"),
        ("start", 1, 1, 2, "c"),
        ("compute", ("up", 1, 3)),
        ("start", 0, 2, 3, ""),
        ("compute", ("up", 1, 4)),
        ("finish", 1, 0, 1, "c"),
        ("start", 2, 0, 1, "c"),
        ("finish", 1, 0, 1, "b"),
        ("start", 2, 0, 1, "b"),
        ("compute", ("out", 1)),
        ("compute", ("score", 1)),
        ("finish", 0, 2, 3, ""),
        ("start", 1, 2, 3, "c"),
        ("start", 1, 2, 3, "b"),
        ("finish", 1, 1, 2, "b"),
        ("start", 2, 1, 2, "b"),
        ("compute", ("head", 1, 0)),
        ("compute", ("head", 1, 1)),
        ("finish", 1, 1, 2, "c"),
        ("start", 2, 1, 2, "c"),
        ("compute", ("head", 1, 2)),
        ("finish", 1, 0, 1, "a"),
        ("start", 1, 2, 3, "a"),
        ("start", 2, 0, 1, "a"),
        ("compute", ("head", 1, 3)),
        ("compute", ("qkv", 1, 0)),
        ("finish", 2, 0, 1, "c"),
        ("finish", 2, 0, 1, "b"),
        ("compute", ("qkv", 1, 1)),
        ("compute", ("qkv", 1, 2)),
        ("start", 0, 3, 4, ""),
        ("finish", 1, 2, 3, "b"),
        ("start", 2, 2, 3, "b"),
        ("finish", 1, 1, 2, "a"),
        ("start", 2, 1, 2, "a"),
        ("compute", ("qkv", 1, 3)),
        ("finish", 2, 1, 2, "b"),
        ("compute", ("down", 0, 0)),
        ("finish", 0, 3, 4, ""),
        ("start", 1, 3, 4, "a"),
        ("start", 1, 3, 4, "b"),
        ("start", 1, 3, 4, "c"),
        ("finish", 2, 0, 1, "a"),
        ("compute", ("down", 0, 1)),
        ("start", 0, 4, 5, ""),
        ("finish", 1, 2, 3, "c"),
        ("start", 2, 2, 3, "c"),
        ("finish", 2, 1, 2, "c"),
        ("compute", ("up", 0, 0)),
        ("finish", 2, 2, 3, "b"),
        ("compute", ("up", 0, 1)),
        ("finish", 1, 2, 3, "a"),
        ("start", 3, 0, 3, "b"),
        ("start", 2, 2, 3, "a"),
        ("finish", 0, 4, 5, ""),
        ("start", 1, 4, 5, "a"),
        ("start", 1, 4, 5, "c"),
        ("start", 1, 4, 5, "b"),
        ("finish", 2, 1, 2, "a"),
        ("compute", ("up", 0, 2)),
        ("compute", ("up", 0, 3)),
        ("start", 0, 5, 6, ""),
        ("finish", 1, 3, 4, "b"),
        ("start", 2, 3, 4, "b"),
        ("compute", ("up", 0, 4)),
        ("finish", 1, 3, 4, "c"),
        ("start", 2, 3, 4, "c"),
        ("finish", 2, 2, 3, "c"),
        ("compute", ("out", 0)),
        ("finish", 0, 5, 6, ""),
        ("start", 1, 5, 6, "b"),
        ("start", 1, 5, 6, "c"),
        ("compute", ("score", 0)),
        ("compute", ("head", 0, 0)),
        ("finish", 1, 4, 5, "c"),
        ("start", 2, 4, 5, "c"),
        ("compute", ("head", 0, 1)),
        ("finish", 2, 2, 3, "a"),
        ("start", 3, 0, 3, "a"),
        ("finish", 2, 3, 4, "b"),
        ("finish", 1, 4, 5, "b"),
        ("start", 2, 4, 5, "b"),
        ("finish", 3, 0, 3, "b"),
        ("start", 4, 0, 3, "b"),
        ("compute", ("head", 0, 2)),
        ("finish", 1, 3, 4, "a"),
        ("start", 2, 3, 4, "a"),
        ("start", 3, 0, 3, "c"),
        ("start", 1, 5, 6, "a"),
        ("finish", 2, 3, 4, "c"),
        ("compute", ("head", 0, 3)),
        ("finish", 1, 5, 6, "b"),
        ("compute", ("qkv", 0, 0)),
        ("compute", ("qkv", 0, 1)),
        ("compute", ("qkv", 0, 2)),
        ("start", 0, 6, 7, ""),
        ("compute", ("qkv", 0, 3)),
        ("finish", 1, 4, 5, "a"),
        ("start", 2, 4, 5, "a"),
        ("compute", "input"),
        ("start", 7, 0, 1, ""),
        ("compute", "embed"),
        ("finish", 0, 6, 7, ""),
        ("start", 1, 6, 7, "a"),
        ("start", 1, 6, 7, "c"),
        ("start", 1, 6, 7, "b"),
        ("finish", 2, 3, 4, "a"),
        ("finish", 7, 0, 1, ""),
        ("finish", 2, 4, 5, "c"),
        ("finish", 1, 5, 6, "c"),
        ("start", 2, 5, 6, "b"),
        ("start", 2, 5, 6, "c"),
        ("finish", 3, 0, 3, "c"),
        ("start", 4, 0, 3, "c"),
        ("finish", 2, 4, 5, "b"),
        ("finish", 4, 0, 3, "b"),
        ("finish", 3, 0, 3, "a"),
        ("start", 4, 0, 3, "a"),
        ("finish", 2, 5, 6, "b"),
        ("finish", 2, 4, 5, "a"),
        ("start", 3, 3, 5, "a"),
        ("finish", 2, 5, 6, "c"),
        ("finish", 1, 5, 6, "a"),
        ("start", 7, 1, 2, ""),
        ("start", 3, 3, 5, "b"),
        ("start", 2, 5, 6, "a"),
        ("finish", 4, 0, 3, "c"),
        ("finish", 1, 6, 7, "c"),
        ("start", 2, 6, 7, "c"),
        ("finish", 1, 6, 7, "b"),
        ("start", 2, 6, 7, "b"),
        ("finish", 1, 6, 7, "a"),
        ("start", 2, 6, 7, "a"),
        ("start", 3, 5, 6, "c"),
        ("start", 3, 3, 5, "c"),
        ("start", 3, 5, 6, "b"),
        ("finish", 4, 0, 3, "a"),
        ("start", 5, 0, 3, ""),
        ("finish", 7, 1, 2, ""),
        ("finish", 3, 3, 5, "b"),
        ("start", 4, 3, 5, "b"),
        ("finish", 2, 5, 6, "a"),
        ("start", 7, 2, 3, ""),
        ("start", 3, 5, 6, "a"),
        ("finish", 3, 5, 6, "c"),
        ("start", 4, 5, 6, "c"),
        ("finish", 3, 5, 6, "b"),
        ("start", 4, 5, 6, "b"),
        ("finish", 3, 3, 5, "c"),
        ("start", 4, 3, 5, "c"),
        ("finish", 3, 3, 5, "a"),
        ("start", 4, 3, 5, "a"),
        ("finish", 2, 6, 7, "a"),
        ("start", 3, 6, 7, "a"),
        ("finish", 2, 6, 7, "c"),
        ("start", 3, 6, 7, "c"),
        ("finish", 2, 6, 7, "b"),
        ("start", 3, 6, 7, "b"),
        ("finish", 4, 3, 5, "b"),
        ("finish", 4, 5, 6, "c"),
        ("finish", 3, 5, 6, "a"),
        ("start", 4, 5, 6, "a"),
        ("finish", 4, 5, 6, "b"),
        ("finish", 7, 2, 3, ""),
        ("start", 7, 3, 4, ""),
        ("finish", 4, 3, 5, "c"),
        ("finish", 3, 6, 7, "c"),
        ("start", 4, 6, 7, "c"),
        ("finish", 3, 6, 7, "b"),
        ("start", 4, 6, 7, "b"),
        ("finish", 3, 6, 7, "a"),
        ("start", 4, 6, 7, "a"),
        ("finish", 4, 3, 5, "a"),
        ("start", 5, 3, 5, ""),
        ("finish", 5, 0, 3, ""),
        ("start", 6, 0, 3, ""),
        ("finish", 4, 5, 6, "a"),
        ("start", 5, 5, 6, ""),
        ("finish", 6, 0, 3, ""),
        ("finish", 4, 6, 7, "c"),
        ("finish", 4, 6, 7, "b"),
        ("finish", 7, 3, 4, ""),
        ("start", 7, 4, 5, ""),
        ("finish", 4, 6, 7, "a"),
        ("start", 5, 6, 7, ""),
        ("finish", 5, 3, 5, ""),
        ("start", 6, 3, 5, ""),
        ("finish", 5, 5, 6, ""),
        ("start", 6, 5, 6, ""),
        ("finish", 5, 6, 7, ""),
        ("start", 6, 6, 7, ""),
        ("finish", 6, 3, 5, ""),
        ("finish", 6, 5, 6, ""),
        ("finish", 7, 4, 5, ""),
        ("finish", 6, 6, 7, ""),
    )


def per_device(rem, plan, pieces, counts, groups, table, again, wqkv, wout, abias, fgain, wup, ubias, wdown, dbias, egain, wpool, pbias, cot):
    pieces = jnp.transpose(pieces, (1, 0, 2))
    slots, entries, width = pieces.shape
    hidden = wup.shape[2]
    layers = wqkv.shape[0]
    token_rows = entries * slots
    vmem = pl.BlockSpec(memory_space=pltpu.VMEM)
    hbm = pl.BlockSpec(memory_space=pl.ANY)
    tile = (PIECE, width)

    def buffers(part):
        quanta, dims = PARTS[part]
        size = quanta.stop - quanta.start
        return [pltpu.VMEM((GROUPS_OUT, size) + (2,) * (3 - k) + tile, BF16) for k in range(4)]

    def body(*refs):
        refs = list(refs)
        fixed = 17 + 4 + 25
        head, rest = refs[: fixed], refs[fixed:]
        parts = [rest[4 * k : 4 * k + 4] for k in range(3)]
        kernel(rem, plan, *head, *parts, *rest[12:])

    copies = len({item[1:] for item in plan if item[0] == "start"})
    scratch = [
        pltpu.VMEM(wqkv.shape, BF16), pltpu.VMEM(wout.shape, BF16), pltpu.VMEM(wup.shape, BF16), pltpu.VMEM(wdown.shape, BF16),
        pltpu.VMEM(wpool.shape, BF16), pltpu.VMEM((width, 128), BF16), pltpu.VMEM((slots, 128, width), BF16),
        pltpu.VMEM((token_rows, width), F32), pltpu.VMEM((2 * layers, token_rows, width), BF16),
        pltpu.VMEM((token_rows, width), BF16), pltpu.VMEM((layers, token_rows, 3 * width), BF16), pltpu.VMEM((layers, token_rows, 128), F32),
        pltpu.VMEM((layers, token_rows, width), BF16), pltpu.VMEM((layers, token_rows, hidden), BF16), pltpu.VMEM((layers, token_rows, hidden), BF16),
        pltpu.VMEM((token_rows, width), BF16), pltpu.VMEM((token_rows, hidden), BF16), pltpu.VMEM((token_rows, 128), BF16), pltpu.VMEM((slots * token_rows, width), BF16), pltpu.VMEM((token_rows, width), F32),
        pltpu.VMEM((width, token_rows), BF16), pltpu.VMEM((entries, width), F32), pltpu.VMEM((entries, width), F32),
        pltpu.VMEM((SLOTS, 4, 2, 2, 2, 2, 2) + tile, BF16), pltpu.VMEM((GROUPS_OUT, 4, 2, 2, 2, 2) + tile, BF16),
        *buffers("a"), *buffers("b"), *buffers("c"),
        pltpu.VMEM((GROUPS_OUT, 4, 2, 2) + tile, BF16), pltpu.VMEM((11, 32, width), F32),
        pltpu.SemaphoreType.DMA((4 * layers + 1,)), pltpu.SemaphoreType.DMA((copies,)), pltpu.SemaphoreType.DMA((copies,)), pltpu.SemaphoreType.DMA,
    ]
    emb, dx, fin, small = pl.pallas_call(
        body,
        out_shape=(
            jax.ShapeDtypeStruct((entries, wpool.shape[1]), BF16),
            jax.ShapeDtypeStruct(pieces.shape, BF16),
            jax.ShapeDtypeStruct((GROUPS_OUT, 4, 2, 2) + tile, BF16),
            jax.ShapeDtypeStruct((32, width), F32),
        ),
        in_specs=[vmem] * 12 + [hbm] * 5,
        out_specs=(vmem, vmem, hbm, vmem),
        scratch_shapes=scratch,
        compiler_params=pltpu.CompilerParams(collective_id=0, has_side_effects=True, vmem_limit_bytes=64 * 2**20),
    )(
        pieces, counts.reshape(1, -1), groups.reshape(1, -1), table, again, abias, fgain, ubias, dbias,
        egain, pbias, cot, wqkv, wout, wup, wdown, wpool,
    )
    return emb, dx, fin, small


def unpack_kernel(rem, fin, small, emb, dx, emb_o, dx_o, table_o, again_o, qkv_o, out_o, abias_o, fgain_o, up_o, ubias_o, down_o, dbias_o, egain_o, pool_o, pbias_o):
    part = lax.axis_index("dp") // rem
    width = fin.shape[-1]
    short = width // SHARDS
    emb_o[...] = emb[...]
    dx_o[...] = dx[...]

    def block(group, k):
        return fin[group, k].reshape(4 * PIECE, width).astype(F32)

    def columns(target, group, count):
        for k in range(count):
            target[..., k * width : (k + 1) * width] = block(group, k)

    def share(value):
        return pltpu.roll(value, width - part * short, 1)[:, 0:short]

    columns(pool_o, 0, 4)
    for layer in range(2):
        down, up, attn = (4, 5, 6) if layer == 0 else (1, 2, 3)
        for k in range(4):
            down_o[layer, k * 64 : (k + 1) * 64, :] = block(down, k)
        columns(up_o.at[layer], up, 4)
        columns(qkv_o.at[layer], attn, 3)
        out_o[layer] = block(attn, 3)
        for row, target in enumerate((again_o, abias_o, fgain_o, dbias_o)):
            target[layer : layer + 1, :] = share(small[8 * layer + row : 8 * layer + row + 1, :])
    half = width // 2

    def long_share(first):
        value = small[pl.ds(first + part // 2, 1), :]
        return jnp.where(part % 2 == 0, value[:, 0:half], value[:, half:width])

    for layer in range(2):
        ubias_o[layer : layer + 1, :] = long_share(8 * layer + 4)
    table_o[...] = share(small[24:32, :])
    egain_o[...] = share(small[16:17, :])
    pbias_o[...] = long_share(17)


def unpack(rem, emb, dx, fin, small):
    width = fin.shape[-1]
    short = width // SHARDS

    def f32(*shape):
        return jax.ShapeDtypeStruct(shape, F32)

    emb, dx, *grads = pl.pallas_call(
        functools.partial(unpack_kernel, rem),
        out_shape=(
            jax.ShapeDtypeStruct(emb.shape, BF16), jax.ShapeDtypeStruct(dx.shape, BF16), f32(8, short), f32(2, short), f32(2, 64, 3 * width),
            f32(2, 64, width), f32(2, short), f32(2, short), f32(2, 64, 4 * width), f32(2, 4 * short), f32(2, 256, width), f32(2, short),
            f32(1, short), f32(64, 4 * width), f32(1, 4 * short),
        ),
        compiler_params=pltpu.CompilerParams(vmem_limit_bytes=64 * 2**20),
    )(fin, small, emb, dx)
    grads[10] = grads[10].reshape(-1)
    grads[12] = grads[12].reshape(-1)
    if rem > 1:
        blocks = [list(range(k * rem, (k + 1) * rem)) for k in range(SHARDS)]
        dims = (1,) * 10 + (0,) * 3
        grads = [
            lax.psum_scatter(g, "dp", scatter_dimension=d, axis_index_groups=blocks, tiled=True)
            for g, d in zip(grads, dims)
        ]
    return (emb, jnp.transpose(dx, (1, 0, 2)), *grads)


def solution(mesh):
    rem = mesh.shape["dp"] // SHARDS
    plan = plan_of()

    def whole(*args):
        return unpack(rem, *per_device(rem, plan, *args))

    placed = (P(("dp", "section"), None, None), P(("dp", "section")), P(("dp", "section"))) + (P(),) * 13 + (P(("dp", "section"), None),)
    return jax.shard_map(
        whole,
        mesh=mesh,
        in_specs=placed,
        out_specs=(
            P(("dp", "section"), None), P(("dp", "section"), None, None), P(None, "dp"), P(None, "dp"), P(None, "dp", None), P(None, "dp", None),
            P(None, "dp"), P(None, "dp"), P(None, "dp", None), P(None, "dp"), P(None, "dp", None), P(None, "dp"), P("dp"), P("dp", None), P("dp"),
        ),
        check_vma=False,
    )
```

```python
import functools

import jax
import jax.numpy as jnp
from jax import lax
from jax.experimental import pallas as pl
from jax.experimental.pallas import tpu as pltpu
from jax.sharding import PartitionSpec as P

HEADS = 8
EPS = 1e-05
MASKED = -1e30
F32 = jnp.float32
BF16 = jnp.bfloat16
MESH = pl.DeviceIdType.MESH
SHARDS = 8
PIECE = 16
GROUPS_OUT = 7
SLOTS = 3


def mm(left, right):
    return jnp.dot(left, right, preferred_element_type=F32)


def mm_right(left, right):
    return lax.dot_general(left, right, (((1,), (1,)), ((), ())), preferred_element_type=F32)


def flipped(value, mask):
    return value + mask - 2 * mask * ((value // mask) % 2)


def normalised(values):
    centre = values - jnp.mean(values, axis=-1, keepdims=True)
    scale = lax.rsqrt(jnp.mean(centre * centre, axis=-1, keepdims=True) + EPS)
    return centre * scale, scale


def gelu_both(v):
    size = jnp.abs(v)
    base = 1.0 + (0.3275911 * 0.7071067811865476) * size
    t = 1.0 / base
    bell = jnp.exp(-0.5 * (v * v))
    poly = t * (
        0.127414796
        + t * (-0.142248368 + t * (0.7107068705 + t * (-0.7265760135 + t * 0.5307027145)))
    )
    tail = poly * bell
    cdf = jnp.where(v >= 0, 1.0 - tail, tail)
    return v * cdf, cdf + v * (bell * 0.3989422804014327)


PARTS = {
    "a": (slice(0, 2), ("x", "y", "zl", "zh")),
    "b": (slice(2, 3), ("y", "zl", "x", "zh")),
    "c": (slice(3, 4), ("zl", "zh", "x", "y")),
}
OTHER = {("c", 6): ("y", "zl", "x", "zh")}
AXES = ("y", "zh", "zl", "x")


def kernel(rem, plan, *refs):
    (
        pieces_ref, counts_ref, groups_ref, table_ref, again_ref, abias_ref, fgain_ref, ubias_ref, dbias_ref,
        egain_ref, pbias_ref, cot_ref, wqkv_hbm, wout_hbm, wup_hbm, wdown_hbm, wpool_hbm,
        emb_ref, dx_ref, fin_ref, small_ref,
        wqkv, wout, wup, wdown, wpool, es, ex, x0, hs, nb, qkv, prob, ctx, act, dg, dyb, dqkv, d_scores, pairs, wide, tmp, npool, upool,
        g_buf, r0, ra, rb, rc, f_buf, s_buf, w_sem, send_sem, recv_sem, out_sem,
    ) = refs
    slots, entries, width = pieces_ref.shape
    layers = again_ref.shape[0]
    token_rows = slots * entries
    b = lax.axis_index("dp") // rem
    s = lax.axis_index("section")
    bits = {"zh": b // 4, "zl": (b // 2) % 2, "x": b % 2, "y": s // 2, "core": s % 2}
    dp_mask = {"zh": 4 * rem, "zl": 2 * rem, "x": rem, "y": 0, "core": 0}
    sec_mask = {"zh": 0, "zl": 0, "x": 0, "y": 2, "core": 1}

    def partner(axis):
        d, e = lax.axis_index("dp"), lax.axis_index("section")
        return (
            flipped(d, dp_mask[axis]) if dp_mask[axis] else d,
            flipped(e, sec_mask[axis]) if sec_mask[axis] else e,
        )

    barrier = pltpu.get_barrier_semaphore()
    for axis in bits:
        pl.semaphore_signal(barrier, inc=1, device_id=partner(axis), device_id_type=MESH)

    loads = {}
    order = []
    for layer in range(layers):
        order += [("qkv", layer, wqkv_hbm, wqkv), ("out", layer, wout_hbm, wout), ("up", layer, wup_hbm, wup), ("down", layer, wdown_hbm, wdown)]
    for at, (name, layer, source, target) in enumerate(order):
        loads[name, layer] = pltpu.make_async_copy(source.at[layer], target.at[layer], w_sem.at[at])
        loads[name, layer].start()
    loads["pool", 0] = pltpu.make_async_copy(wpool_hbm, wpool, w_sem.at[len(order)])
    loads["pool", 0].start()

    def ready(name, layer):
        loads.pop((name, layer)).wait()

    def rows(j):
        return pl.ds(pl.multiple_of(j * entries, entries), entries)

    def column(row_ref):
        eye = lax.broadcasted_iota(jnp.int32, (entries, entries), 0) == lax.broadcasted_iota(
            jnp.int32, (entries, entries), 1
        )
        row = row_ref[...].astype(F32)
        return jnp.sum(jnp.where(eye, row, 0.0), axis=1, keepdims=True)

    count = column(counts_ref)
    group = column(groups_ref)

    head_of = lax.broadcasted_iota(jnp.int32, (width, 128), 0) // (width // HEADS)
    lane_of = lax.broadcasted_iota(jnp.int32, (width, 128), 1) % 64
    head_of_t = lax.broadcasted_iota(jnp.int32, (128, width), 1) // (width // HEADS)
    lane_of_t = lax.broadcasted_iota(jnp.int32, (128, width), 0)
    scaling = (width // HEADS) ** -0.5
    lane_slot = (lax.broadcasted_iota(jnp.int32, (token_rows, 128), 1) % 64) // HEADS
    es[...] = jnp.where(lane_of % HEADS == head_of, scaling, 0.0).astype(BF16)
    for j in range(slots):
        ex[j] = jnp.where(lane_of_t - head_of_t == j * HEADS, 1.0, 0.0).astype(BF16)
    live_lanes = (
        (lax.broadcasted_iota(jnp.int32, (entries, 128), 1) % 64) // HEADS
    ).astype(F32) < count

    group_rows = jnp.zeros((entries, width), F32)
    for g in range(table_ref.shape[0]):
        group_rows = jnp.where(group == g, table_ref[g : g + 1, :].astype(F32), group_rows)
    for j in range(slots):
        x0[j * entries : (j + 1) * entries, :] = pieces_ref[j].astype(F32) + group_rows

    def norm_rows(source, gain):
        for j in range(slots):
            n, _r = normalised(source[rows(j), :].astype(F32))
            nb[rows(j), :] = (n * gain).astype(BF16)

    def rolled(value, op):
        for shift in (8, 16, 32):
            value = op(value, pltpu.roll(value, shift, 1))
        return value

    def spread_rows(block, value):
        n = value.shape[-1]
        return (value.reshape(slots, entries, n) * block[None]).reshape(token_rows, n)

    def pair_sums(key_rows, query_rows):
        for j in range(slots):
            pairs[j * token_rows : (j + 1) * token_rows, :] = spread_rows(key_rows[rows(j), :], query_rows)
        sums = mm(pairs[...], es[...])
        total = jnp.zeros((token_rows, 128), F32)
        for j in range(slots):
            total = jnp.where(lane_slot == j, sums[j * token_rows : (j + 1) * token_rows, :], total)
        return total

    def attention_forward(layer, source, target):
        norm_rows(source, again_ref[layer : layer + 1, :].astype(F32))
        ready("qkv", layer)
        for t in range(3):
            cols = pl.ds(t * width, width)
            qkv[layer, :, cols] = mm(nb[...], wqkv[layer, :, cols]).astype(BF16)
        scores = pair_sums(qkv.at[layer, :, pl.ds(width, width)], qkv[layer, :, 0:width])
        scores = jnp.where(live_lanes[None], scores.reshape(slots, entries, 128), MASKED).reshape(token_rows, 128)
        raised = jnp.exp(scores - rolled(scores, jnp.maximum))
        p = raised / rolled(raised, jnp.add)
        prob[layer] = p
        p_low = p.astype(BF16)

        @pl.loop(0, width // 128)
        def _(c):
            lanes = pl.ds(pl.multiple_of(c * 128, 128), 128)
            v_lanes = pl.ds(pl.multiple_of(2 * width + c * 128, 128), 128)
            total = jnp.zeros((token_rows, 128), F32)
            for j in range(slots):
                total += spread_rows(qkv[layer, rows(j), v_lanes].astype(F32), mm(p_low, ex[j, :, lanes]))
            ctx[layer, :, lanes] = total.astype(BF16)

        ready("out", layer)
        bias = abias_ref[layer : layer + 1, :].astype(F32)
        hs[target] = (source[...].astype(F32) + mm(ctx[layer], wout[layer]) + bias).astype(BF16)

    def ffn_forward(layer, source, target):
        norm_rows(source, fgain_ref[layer : layer + 1, :].astype(F32))
        ready("up", layer)
        ready("down", layer)
        wide[...] = source[...].astype(F32) + dbias_ref[layer : layer + 1, :].astype(F32)
        for t in range(wup.shape[2] // 256):
            cols = pl.ds(t * 256, 256)
            inner = mm(nb[...], wup[layer, :, cols]) + ubias_ref[layer : layer + 1, cols].astype(F32)
            activated, slope = gelu_both(inner)
            act[layer, :, cols] = activated.astype(BF16)
            dg[layer, :, cols] = slope.astype(BF16)
            wide[...] += mm(activated.astype(BF16), wdown[layer, cols, :])
        hs[target] = wide[...].astype(BF16)

    def put_columns(slot, quantum, value):
        block = value.astype(BF16)
        for o in range(SHARDS):
            for y in range(2):
                for c in range(2):
                    at = o * 64 + y * 32 + c * PIECE
                    g_buf[slot, quantum, c, y, o // 4, (o // 2) % 2, o % 2] = block[at : at + PIECE]

    def put_down(slot, t, value):
        block = value.astype(BF16)
        for half in range(2):
            for k in range(4):
                for y in range(2):
                    for c in range(2):
                        at = half * 256 + k * 64 + y * 32 + c * PIECE
                        g_buf[slot, k, c, y, t // 2, t % 2, half] = block[at : at + PIECE]

    def col_sum(value):
        return jnp.sum(value, axis=0, keepdims=True)

    part_buffers = {"a": ra, "b": rb, "c": rc}
    copies = sorted({item[1:] for item in plan if item[0] == "start"})
    written = []

    def views_of(stage, lo, hi, part):
        core, y = bits["core"], bits["y"]
        if stage == 0:
            slot = lo % SLOTS
            return "core", g_buf.at[slot, :, 1 - core], g_buf.at[slot, :, core], r0.at[lo]
        if stage <= 4:
            quanta, dims = PARTS[part][0], OTHER.get((part, lo), PARTS[part][1])
            axis = dims[stage - 1]
            left = [a for a in AXES if a not in dims[: stage - 1]]
            buffers = part_buffers[part]
            lead = (slice(lo, hi), quanta if stage == 1 else slice(None))
            before = r0 if stage == 1 else buffers[stage - 2]

            def half(index):
                return before.at[lead + tuple(index if a == axis else slice(None) for a in left)]

            return axis, half(1 - bits[axis]), half(bits[axis]), buffers[stage - 1].at[lo:hi]
        if stage == 5:
            view = f_buf.at[lo:hi, :, y, core]
            return "y", view, None, view
        if stage == 6:
            view = f_buf.at[lo:hi, :, :, core]
            return "core", view, None, view
        return ("core", "x", "y", "zl", "zh")[lo], s_buf.at[2 * lo], s_buf.at[2 * lo], s_buf.at[2 * lo + 1]

    def copy_of(key):
        axis, source, mine, landing = views_of(*key)
        at = copies.index(key)
        return pltpu.make_async_remote_copy(
            src_ref=source,
            dst_ref=landing,
            send_sem=send_sem.at[at],
            recv_sem=recv_sem.at[at],
            device_id=partner(axis),
            device_id_type=MESH,
        )

    def start(*key):
        copy_of(key).start()

    def finish(*key):
        stage, lo, hi, part = key
        axis, source, mine, landing = views_of(*key)
        copy_of(key).wait()
        if stage < 4:
            landing[...] = landing[...] + mine[...]
        elif stage == 4:
            f_buf[lo:hi, PARTS[part][0], bits["y"], bits["core"]] = landing[...] + mine[...]
        elif stage == 6:
            written.append(pltpu.make_async_copy(f_buf.at[lo:hi], fin_ref.at[lo:hi], out_sem.at[lo]))
            written[-1].start()
        elif stage == 7:
            s_buf[2 * lo + 2] = landing[...] + mine[...]

    def put_small(at, value):
        s_buf[0, pl.ds(at, value.shape[0]), :] = value

    def forward_attention(layer):
        attention_forward(layer, x0 if layer == 0 else hs.at[2 * layer - 1], 2 * layer)

    def forward_feed(layer):
        ffn_forward(layer, hs.at[2 * layer], 2 * layer + 1)

    def pool_forward():
        live_sum = jnp.zeros((entries, width), F32)
        for j in range(slots):
            n, _r = normalised(hs[2 * layers - 1, rows(j), :].astype(F32))
            live_sum += jnp.where(count > j, n, 0.0)
        npool[...] = live_sum / count
        pooled = (npool[...] * egain_ref[...].astype(F32).reshape(1, width)).astype(BF16)
        pooled_t = pooled.astype(F32).T.astype(BF16)
        ready("pool", 0)
        for k in range(4):
            put_columns(0, k, mm(pooled_t, cot_ref[:, k * width : (k + 1) * width]))

    def embed():
        pooled = (npool[...] * egain_ref[...].astype(F32).reshape(1, width)).astype(BF16)
        for k in range(4):
            cols = slice(k * width, (k + 1) * width)
            emb_ref[:, cols] = (mm(pooled, wpool[:, cols]) + pbias_ref[cols].astype(F32).reshape(1, width)).astype(BF16)

    def pool_backward():
        for k in range(4):
            put_small(17 + k, col_sum(cot_ref[:, k * width : (k + 1) * width].astype(F32)))
        d_pooled = mm_right(cot_ref[...], wpool[...]).astype(BF16).astype(F32)
        put_small(16, col_sum(d_pooled * npool[...]))
        upool[...] = d_pooled * egain_ref[...].astype(F32).reshape(1, width) / count
        for j in range(slots):
            n, r = normalised(hs[2 * layers - 1, rows(j), :].astype(F32))
            u = jnp.where(count > j, upool[...], 0.0)
            d = r * (u - jnp.mean(u, axis=-1, keepdims=True) - n * jnp.mean(u * n, axis=-1, keepdims=True))
            dyb[rows(j), :] = d.astype(BF16)

    def norm_backward(source, gain, at, keep_wide):
        total = jnp.zeros((entries, width), F32)
        for j in range(slots):
            n, r = normalised(source[rows(j), :].astype(F32))
            d_normed = wide[rows(j), :]
            u = d_normed * gain
            d = r * (u - jnp.mean(u, axis=-1, keepdims=True) - n * jnp.mean(u * n, axis=-1, keepdims=True))
            d_h = dyb[rows(j), :].astype(F32) + d
            dyb[rows(j), :] = d_h.astype(BF16)
            if keep_wide:
                wide[rows(j), :] = d_h
            total += d_normed * n
        put_small(at, col_sum(total))

    def dy_sum(at):
        put_small(at, col_sum(dyb[...].astype(F32)))

    def turned(value):
        return value.astype(F32).T.astype(BF16)

    def down_grad(layer, slot, part):
        if part == 0:
            dy_sum(8 * layer + 3)
        for t in (2 * part, 2 * part + 1):
            cols = pl.ds(t * width, width)
            put_down(slot, t, mm(turned(act[layer, :, cols]), dyb[...]))

    def up_grad(layer, slot, source, t):
        gain = fgain_ref[layer : layer + 1, :].astype(F32)
        if t == 0:
            norm_rows(source, gain)
            tmp[...] = turned(nb[...])
        if t < 4:
            cols = pl.ds(t * width, width)
            d_act = mm_right(dyb[...], wdown[layer, cols, :])
            d_inner = (d_act * dg[layer, :, cols].astype(F32)).astype(BF16)
            put_small(8 * layer + 4 + t, col_sum(d_inner.astype(F32)))
            put_columns(slot, t, mm(tmp[...], d_inner))
            dqkv[:, cols] = d_inner
        else:
            wide[...] = mm_right(dqkv[...], wup[layer])
            norm_backward(source, gain, 8 * layer + 2, False)

    def out_grad(layer, slot):
        dy_sum(8 * layer + 1)
        put_columns(slot, 3, mm(turned(ctx[layer]), dyb[...]))
        nb[...] = mm_right(dyb[...], wout[layer]).astype(BF16)

    def score_grad(layer):
        d_prob = pair_sums(qkv.at[layer, :, pl.ds(2 * width, width)], nb[...]) * (1.0 / scaling)
        p = prob[layer]
        mixed = p * d_prob
        d_scores[...] = (mixed - p * rolled(mixed, jnp.add)).astype(BF16)

    def head_grad(layer, c):
        def lanes(part):
            return pl.ds(part * width + c * 128, 128)

        p_low = prob[layer].astype(BF16)
        d_q = jnp.zeros((token_rows, 128), F32)
        for j in range(slots):
            weights = mm(p_low, ex[j, :, lanes(0)])
            d_v = jnp.sum((weights * nb[:, lanes(0)].astype(F32)).reshape(slots, entries, 128), axis=0)
            weights = mm(d_scores[...], ex[j, :, lanes(0)])
            d_q += spread_rows(qkv[layer, rows(j), lanes(1)].astype(F32), weights)
            d_k = jnp.sum((weights * qkv[layer, :, lanes(0)].astype(F32)).reshape(slots, entries, 128), axis=0)
            dqkv[rows(j), lanes(1)] = (d_k * scaling).astype(BF16)
            dqkv[rows(j), lanes(2)] = d_v.astype(BF16)
        dqkv[:, lanes(0)] = (d_q * scaling).astype(BF16)

    def qkv_grad(layer, slot, source, t):
        gain = again_ref[layer : layer + 1, :].astype(F32)
        if t == 0:
            norm_rows(source, gain)
            tmp[...] = turned(nb[...])
        if t < 3:
            put_columns(slot, t, mm(tmp[...], dqkv[:, t * width : (t + 1) * width]))
        else:
            wide[...] = mm_right(dqkv[:, 0 : 3 * width], wqkv[layer])
            norm_backward(source, gain, 8 * layer, layer == 0)

    def finish_input():
        sums = jnp.zeros((entries, width), F32)
        for j in range(slots):
            sums += wide[j * entries : (j + 1) * entries, :]
            dx_ref[j] = wide[j * entries : (j + 1) * entries, :].astype(BF16)
        for g in range(table_ref.shape[0]):
            put_small(24 + g, col_sum(jnp.where(group == g, sums, 0.0)))

    s_buf[0] = jnp.zeros(s_buf.shape[1:], F32)

    computations = {
        "af0": lambda: forward_attention(0),
        "ff0": lambda: forward_feed(0),
        "af1": lambda: forward_attention(1),
        "ff1": lambda: forward_feed(1),
        "pool": pool_forward,
        "embed": embed,
        "pool_backward": pool_backward,
        "input": finish_input,
    }
    for layer in range(layers):
        first = 1 if layer == 1 else 4
        feed_source = hs.at[2 * layer]
        attn_source = hs.at[1] if layer == 1 else x0
        down, up, attn = (first % SLOTS, (first + 1) % SLOTS, (first + 2) % SLOTS)
        for t in range(2):
            computations["down", layer, t] = functools.partial(down_grad, layer, down, t)
        for t in range(5):
            computations["up", layer, t] = functools.partial(up_grad, layer, up, feed_source, t)
        computations["out", layer] = functools.partial(out_grad, layer, attn)
        computations["score", layer] = functools.partial(score_grad, layer)
        for t in range(4):
            computations["head", layer, t] = functools.partial(head_grad, layer, t)
            computations["qkv", layer, t] = functools.partial(qkv_grad, layer, attn, attn_source, t)
    entered = all(p[0] == "compute" for p in plan)
    if entered:
        pl.semaphore_wait(barrier, 5)
    for item in plan:
        if item[0] == "compute":
            computations[item[1]]()
            continue
        if not entered:
            pl.semaphore_wait(barrier, 5)
            entered = True
        if item[0] == "start":
            start(*item[1:])
        elif item[0] == "finish":
            finish(*item[1:])
    for copy in loads.values():
        copy.wait()
    small_ref[...] = s_buf[10]
    for copy in written:
        copy.wait()


def plan_of():
    return (
        ("compute", "af0"),
        ("compute", "ff0"),
        ("compute", "af1"),
        ("compute", "ff1"),
        ("compute", "pool"),
        ("start", 0, 0, 1, ""),
        ("compute", "pool_backward"),
        ("compute", ("down", 1, 0)),
        ("compute", ("down", 1, 1)),
        ("start", 0, 1, 2, ""),
        ("finish", 0, 0, 1, ""),
        ("start", 1, 0, 1, "a"),
        ("start", 1, 0, 1, "b"),
        ("start", 1, 0, 1, "c"),
        ("compute", ("up", 1, 0)),
        ("compute", ("up", 1, 1)),
        ("compute", ("up", 1, 2)),
        ("finish", 0, 1, 2, ""),
        ("start", 1, 1, 2, "a"),
        ("start", 1, 1, 2, "b"),
        ("start", 1, 1, 2, "c"),
        ("compute", ("up", 1, 3)),
        ("start", 0, 2, 3, ""),
        ("compute", ("up", 1, 4)),
        ("finish", 1, 0, 1, "c"),
        ("start", 2, 0, 1, "c"),
        ("finish", 1, 0, 1, "b"),
        ("start", 2, 0, 1, "b"),
        ("compute", ("out", 1)),
        ("compute", ("score", 1)),
        ("finish", 0, 2, 3, ""),
        ("start", 1, 2, 3, "c"),
        ("start", 1, 2, 3, "b"),
        ("finish", 1, 1, 2, "b"),
        ("start", 2, 1, 2, "b"),
        ("compute", ("head", 1, 0)),
        ("compute", ("head", 1, 1)),
        ("finish", 1, 1, 2, "c"),
        ("start", 2, 1, 2, "c"),
        ("compute", ("head", 1, 2)),
        ("finish", 1, 0, 1, "a"),
        ("start", 1, 2, 3, "a"),
        ("start", 2, 0, 1, "a"),
        ("compute", ("head", 1, 3)),
        ("compute", ("qkv", 1, 0)),
        ("finish", 2, 0, 1, "c"),
        ("finish", 2, 0, 1, "b"),
        ("compute", ("qkv", 1, 1)),
        ("compute", ("qkv", 1, 2)),
        ("start", 0, 3, 4, ""),
        ("finish", 1, 2, 3, "b"),
        ("start", 2, 2, 3, "b"),
        ("finish", 1, 1, 2, "a"),
        ("start", 2, 1, 2, "a"),
        ("compute", ("qkv", 1, 3)),
        ("finish", 2, 1, 2, "b"),
        ("compute", ("down", 0, 0)),
        ("finish", 0, 3, 4, ""),
        ("start", 1, 3, 4, "a"),
        ("start", 1, 3, 4, "b"),
        ("start", 1, 3, 4, "c"),
        ("finish", 2, 0, 1, "a"),
        ("compute", ("down", 0, 1)),
        ("start", 0, 4, 5, ""),
        ("finish", 1, 2, 3, "c"),
        ("start", 2, 2, 3, "c"),
        ("finish", 2, 1, 2, "c"),
        ("compute", ("up", 0, 0)),
        ("finish", 2, 2, 3, "b"),
        ("compute", ("up", 0, 1)),
        ("finish", 1, 2, 3, "a"),
        ("start", 3, 0, 3, "b"),
        ("start", 2, 2, 3, "a"),
        ("finish", 0, 4, 5, ""),
        ("start", 1, 4, 5, "a"),
        ("start", 1, 4, 5, "c"),
        ("start", 1, 4, 5, "b"),
        ("finish", 2, 1, 2, "a"),
        ("compute", ("up", 0, 2)),
        ("compute", ("up", 0, 3)),
        ("start", 0, 5, 6, ""),
        ("finish", 1, 3, 4, "b"),
        ("start", 2, 3, 4, "b"),
        ("compute", ("up", 0, 4)),
        ("finish", 1, 3, 4, "c"),
        ("start", 2, 3, 4, "c"),
        ("finish", 2, 2, 3, "c"),
        ("compute", ("out", 0)),
        ("finish", 0, 5, 6, ""),
        ("start", 1, 5, 6, "b"),
        ("start", 1, 5, 6, "c"),
        ("compute", ("score", 0)),
        ("compute", ("head", 0, 0)),
        ("finish", 1, 4, 5, "c"),
        ("start", 2, 4, 5, "c"),
        ("compute", ("head", 0, 1)),
        ("finish", 2, 2, 3, "a"),
        ("start", 3, 0, 3, "a"),
        ("finish", 2, 3, 4, "b"),
        ("finish", 1, 4, 5, "b"),
        ("start", 2, 4, 5, "b"),
        ("finish", 3, 0, 3, "b"),
        ("start", 4, 0, 3, "b"),
        ("compute", ("head", 0, 2)),
        ("finish", 1, 3, 4, "a"),
        ("start", 2, 3, 4, "a"),
        ("start", 3, 0, 3, "c"),
        ("start", 1, 5, 6, "a"),
        ("finish", 2, 3, 4, "c"),
        ("compute", ("head", 0, 3)),
        ("finish", 1, 5, 6, "b"),
        ("compute", ("qkv", 0, 0)),
        ("compute", ("qkv", 0, 1)),
        ("compute", ("qkv", 0, 2)),
        ("start", 0, 6, 7, ""),
        ("compute", ("qkv", 0, 3)),
        ("finish", 1, 4, 5, "a"),
        ("start", 2, 4, 5, "a"),
        ("compute", "input"),
        ("start", 7, 0, 1, ""),
        ("compute", "embed"),
        ("finish", 0, 6, 7, ""),
        ("start", 1, 6, 7, "a"),
        ("start", 1, 6, 7, "c"),
        ("start", 1, 6, 7, "b"),
        ("finish", 2, 3, 4, "a"),
        ("finish", 7, 0, 1, ""),
        ("finish", 2, 4, 5, "c"),
        ("finish", 1, 5, 6, "c"),
        ("start", 2, 5, 6, "b"),
        ("start", 2, 5, 6, "c"),
        ("finish", 3, 0, 3, "c"),
        ("start", 4, 0, 3, "c"),
        ("finish", 2, 4, 5, "b"),
        ("finish", 4, 0, 3, "b"),
        ("finish", 3, 0, 3, "a"),
        ("start", 4, 0, 3, "a"),
        ("finish", 2, 5, 6, "b"),
        ("finish", 2, 4, 5, "a"),
        ("start", 3, 3, 5, "a"),
        ("finish", 2, 5, 6, "c"),
        ("finish", 1, 5, 6, "a"),
        ("start", 7, 1, 2, ""),
        ("start", 3, 3, 5, "b"),
        ("start", 2, 5, 6, "a"),
        ("finish", 4, 0, 3, "c"),
        ("finish", 1, 6, 7, "c"),
        ("start", 2, 6, 7, "c"),
        ("finish", 1, 6, 7, "b"),
        ("start", 2, 6, 7, "b"),
        ("finish", 1, 6, 7, "a"),
        ("start", 2, 6, 7, "a"),
        ("start", 3, 5, 6, "c"),
        ("start", 3, 3, 5, "c"),
        ("start", 3, 5, 6, "b"),
        ("finish", 4, 0, 3, "a"),
        ("start", 5, 0, 3, ""),
        ("finish", 7, 1, 2, ""),
        ("finish", 3, 3, 5, "b"),
        ("start", 4, 3, 5, "b"),
        ("finish", 2, 5, 6, "a"),
        ("start", 7, 2, 3, ""),
        ("start", 3, 5, 6, "a"),
        ("finish", 3, 5, 6, "c"),
        ("start", 4, 5, 6, "c"),
        ("finish", 3, 5, 6, "b"),
        ("start", 4, 5, 6, "b"),
        ("finish", 3, 3, 5, "c"),
        ("start", 4, 3, 5, "c"),
        ("finish", 3, 3, 5, "a"),
        ("start", 4, 3, 5, "a"),
        ("finish", 2, 6, 7, "a"),
        ("start", 3, 6, 7, "a"),
        ("finish", 2, 6, 7, "c"),
        ("start", 3, 6, 7, "c"),
        ("finish", 2, 6, 7, "b"),
        ("start", 3, 6, 7, "b"),
        ("finish", 4, 3, 5, "b"),
        ("finish", 4, 5, 6, "c"),
        ("finish", 3, 5, 6, "a"),
        ("start", 4, 5, 6, "a"),
        ("finish", 4, 5, 6, "b"),
        ("finish", 7, 2, 3, ""),
        ("start", 7, 3, 4, ""),
        ("finish", 4, 3, 5, "c"),
        ("finish", 3, 6, 7, "c"),
        ("start", 4, 6, 7, "c"),
        ("finish", 3, 6, 7, "b"),
        ("start", 4, 6, 7, "b"),
        ("finish", 3, 6, 7, "a"),
        ("start", 4, 6, 7, "a"),
        ("finish", 4, 3, 5, "a"),
        ("start", 5, 3, 5, ""),
        ("finish", 5, 0, 3, ""),
        ("start", 6, 0, 3, ""),
        ("finish", 4, 5, 6, "a"),
        ("start", 5, 5, 6, ""),
        ("finish", 6, 0, 3, ""),
        ("finish", 4, 6, 7, "c"),
        ("finish", 4, 6, 7, "b"),
        ("finish", 7, 3, 4, ""),
        ("start", 7, 4, 5, ""),
        ("finish", 4, 6, 7, "a"),
        ("start", 5, 6, 7, ""),
        ("finish", 5, 3, 5, ""),
        ("start", 6, 3, 5, ""),
        ("finish", 5, 5, 6, ""),
        ("start", 6, 5, 6, ""),
        ("finish", 5, 6, 7, ""),
        ("start", 6, 6, 7, ""),
        ("finish", 6, 3, 5, ""),
        ("finish", 6, 5, 6, ""),
        ("finish", 7, 4, 5, ""),
        ("finish", 6, 6, 7, ""),
    )


def per_device(rem, plan, pieces, counts, groups, table, again, wqkv, wout, abias, fgain, wup, ubias, wdown, dbias, egain, wpool, pbias, cot):
    pieces = jnp.transpose(pieces, (1, 0, 2))
    slots, entries, width = pieces.shape
    hidden = wup.shape[2]
    layers = wqkv.shape[0]
    token_rows = entries * slots
    vmem = pl.BlockSpec(memory_space=pltpu.VMEM)
    hbm = pl.BlockSpec(memory_space=pl.ANY)
    tile = (PIECE, width)

    def buffers(part):
        quanta, dims = PARTS[part]
        size = quanta.stop - quanta.start
        return [pltpu.VMEM((GROUPS_OUT, size) + (2,) * (3 - k) + tile, BF16) for k in range(4)]

    def body(*refs):
        refs = list(refs)
        fixed = 17 + 4 + 25
        head, rest = refs[: fixed], refs[fixed:]
        parts = [rest[4 * k : 4 * k + 4] for k in range(3)]
        kernel(rem, plan, *head, *parts, *rest[12:])

    copies = len({item[1:] for item in plan if item[0] == "start"})
    scratch = [
        pltpu.VMEM(wqkv.shape, BF16), pltpu.VMEM(wout.shape, BF16), pltpu.VMEM(wup.shape, BF16), pltpu.VMEM(wdown.shape, BF16),
        pltpu.VMEM(wpool.shape, BF16), pltpu.VMEM((width, 128), BF16), pltpu.VMEM((slots, 128, width), BF16),
        pltpu.VMEM((token_rows, width), F32), pltpu.VMEM((2 * layers, token_rows, width), BF16),
        pltpu.VMEM((token_rows, width), BF16), pltpu.VMEM((layers, token_rows, 3 * width), BF16), pltpu.VMEM((layers, token_rows, 128), F32),
        pltpu.VMEM((layers, token_rows, width), BF16), pltpu.VMEM((layers, token_rows, hidden), BF16), pltpu.VMEM((layers, token_rows, hidden), BF16),
        pltpu.VMEM((token_rows, width), BF16), pltpu.VMEM((token_rows, hidden), BF16), pltpu.VMEM((token_rows, 128), BF16), pltpu.VMEM((slots * token_rows, width), BF16), pltpu.VMEM((token_rows, width), F32),
        pltpu.VMEM((width, token_rows), BF16), pltpu.VMEM((entries, width), F32), pltpu.VMEM((entries, width), F32),
        pltpu.VMEM((SLOTS, 4, 2, 2, 2, 2, 2) + tile, BF16), pltpu.VMEM((GROUPS_OUT, 4, 2, 2, 2, 2) + tile, BF16),
        *buffers("a"), *buffers("b"), *buffers("c"),
        pltpu.VMEM((GROUPS_OUT, 4, 2, 2) + tile, BF16), pltpu.VMEM((11, 32, width), F32),
        pltpu.SemaphoreType.DMA((4 * layers + 1,)), pltpu.SemaphoreType.DMA((copies,)), pltpu.SemaphoreType.DMA((copies,)), pltpu.SemaphoreType.DMA((GROUPS_OUT,)),
    ]
    emb, dx, fin, small = pl.pallas_call(
        body,
        out_shape=(
            jax.ShapeDtypeStruct((entries, wpool.shape[1]), BF16),
            jax.ShapeDtypeStruct(pieces.shape, BF16),
            jax.ShapeDtypeStruct((GROUPS_OUT, 4, 2, 2) + tile, BF16),
            jax.ShapeDtypeStruct((32, width), F32),
        ),
        in_specs=[vmem] * 12 + [hbm] * 5,
        out_specs=(vmem, vmem, hbm, vmem),
        scratch_shapes=scratch,
        compiler_params=pltpu.CompilerParams(collective_id=0, has_side_effects=True, vmem_limit_bytes=64 * 2**20),
    )(
        pieces, counts.reshape(1, -1), groups.reshape(1, -1), table, again, abias, fgain, ubias, dbias,
        egain, pbias, cot, wqkv, wout, wup, wdown, wpool,
    )
    return emb, dx, fin, small


def unpack_kernel(rem, fin, small, emb, dx, emb_o, dx_o, table_o, again_o, qkv_o, out_o, abias_o, fgain_o, up_o, ubias_o, down_o, dbias_o, egain_o, pool_o, pbias_o):
    part = lax.axis_index("dp") // rem
    width = fin.shape[-1]
    short = width // SHARDS
    emb_o[...] = emb[...]
    dx_o[...] = dx[...]

    def block(group, k):
        return fin[group, k].reshape(4 * PIECE, width).astype(F32)

    def columns(target, group, count):
        for k in range(count):
            target[..., k * width : (k + 1) * width] = block(group, k)

    def share(value):
        return pltpu.roll(value, width - part * short, 1)[:, 0:short]

    columns(pool_o, 0, 4)
    for layer in range(2):
        down, up, attn = (4, 5, 6) if layer == 0 else (1, 2, 3)
        for k in range(4):
            down_o[layer, k * 64 : (k + 1) * 64, :] = block(down, k)
        columns(up_o.at[layer], up, 4)
        columns(qkv_o.at[layer], attn, 3)
        out_o[layer] = block(attn, 3)
        for row, target in enumerate((again_o, abias_o, fgain_o, dbias_o)):
            target[layer : layer + 1, :] = share(small[8 * layer + row : 8 * layer + row + 1, :])
    half = width // 2

    def long_share(first):
        value = small[pl.ds(first + part // 2, 1), :]
        return jnp.where(part % 2 == 0, value[:, 0:half], value[:, half:width])

    for layer in range(2):
        ubias_o[layer : layer + 1, :] = long_share(8 * layer + 4)
    table_o[...] = share(small[24:32, :])
    egain_o[...] = share(small[16:17, :])
    pbias_o[...] = long_share(17)


def unpack(rem, emb, dx, fin, small):
    width = fin.shape[-1]
    short = width // SHARDS

    def f32(*shape):
        return jax.ShapeDtypeStruct(shape, F32)

    emb, dx, *grads = pl.pallas_call(
        functools.partial(unpack_kernel, rem),
        out_shape=(
            jax.ShapeDtypeStruct(emb.shape, BF16), jax.ShapeDtypeStruct(dx.shape, BF16), f32(8, short), f32(2, short), f32(2, 64, 3 * width),
            f32(2, 64, width), f32(2, short), f32(2, short), f32(2, 64, 4 * width), f32(2, 4 * short), f32(2, 256, width), f32(2, short),
            f32(1, short), f32(64, 4 * width), f32(1, 4 * short),
        ),
        compiler_params=pltpu.CompilerParams(vmem_limit_bytes=64 * 2**20),
    )(fin, small, emb, dx)
    grads[10] = grads[10].reshape(-1)
    grads[12] = grads[12].reshape(-1)
    if rem > 1:
        blocks = [list(range(k * rem, (k + 1) * rem)) for k in range(SHARDS)]
        dims = (1,) * 10 + (0,) * 3
        grads = [
            lax.psum_scatter(g, "dp", scatter_dimension=d, axis_index_groups=blocks, tiled=True)
            for g, d in zip(grads, dims)
        ]
    return (emb, jnp.transpose(dx, (1, 0, 2)), *grads)


def solution(mesh):
    rem = mesh.shape["dp"] // SHARDS
    plan = plan_of()

    def whole(*args):
        return unpack(rem, *per_device(rem, plan, *args))

    placed = (P(("dp", "section"), None, None), P(("dp", "section")), P(("dp", "section"))) + (P(),) * 13 + (P(("dp", "section"), None),)
    return jax.shard_map(
        whole,
        mesh=mesh,
        in_specs=placed,
        out_specs=(
            P(("dp", "section"), None), P(("dp", "section"), None, None), P(None, "dp"), P(None, "dp"), P(None, "dp", None), P(None, "dp", None),
            P(None, "dp"), P(None, "dp"), P(None, "dp", None), P(None, "dp"), P(None, "dp", None), P(None, "dp"), P("dp"), P("dp", None), P("dp"),
        ),
        check_vma=False,
    )
```
